32 devices in a mesh: slab: 8 (over z, y), grp: 4 (over x, core).
Axes of the slice: x: 2, y: 2, z: 4, core: 2. Of those that a mesh axis runs over, the one named last changes fastest.
Arguments:
- pencils: float32 [256, 256, 512], P('slab', 'grp'), may hold values from -6 to 6
- send_map: int32 [8, 4, 8, 16], P('slab', 'grp'), may hold values from -1 to 8191, as said below
- interp_index: int32 [2, 8, 8, 256], P(None, 'slab', None, 'grp'), may hold values from 0 to 127, as said below
- interp_frac: float32 [8, 8, 256], P('slab', None, 'grp'), may hold values from 0 to 1
- ori_count: int32 [8], P('slab'), may hold values from 1 to 8, as said below
- spectra: bfloat16 [64, 256, 512], P('slab', 'grp'), may hold values from -6 to 6
- class_ids: int32 [64], P('slab'), may hold values from 0 to 15
- ctf_table: bfloat16 [16, 256, 256], P(None, 'grp'), may hold values from -1 to 1
Outputs:
- scores: float32 [64, 512], P('slab', 'grp')
The draws below stay inside these ranges and needn't reach their ends.
Inputs may be any that keep to these rules, and one draw needn't show every extreme that they name: `send_map`: slots with index 16 or more are never used; for every row group and owner, the used slots of one source come first, at least one, and one source fills all 16. `interp_index`: every entry names a slot that send_map fills for that owner and row group. `ori_count`: some owner lists 8 orientations.
All inputs are finite; a program needn't handle non-finite values.
Results may differ from the reference program's by a relative error of at most 0.005.
Values may be sent and summed in bfloat16 or wider, within the bound.
A program may use at most 64 MiB of HBM per device.

```python
import math
import jax
import jax.numpy as jnp
from jax import lax

NF = 256
CAP = 16
ORI_MAX = 8
TSIDE = 8
CLASSES = 16
PART_DEV = 8
PARTICLES = 64
SLAB_ROWS = 8192
SLOTS = 128
TRANS = 64
N_SLAB = 8
N_GRP = 4


def slot_counts(key):
    key_fill = jax.random.fold_in(key, 101)
    key_hot = jax.random.fold_in(key, 102)
    filled = jax.random.randint(key_fill, (N_SLAB, N_GRP, N_SLAB), 1, CAP + 1)
    hottest = jax.random.randint(key_hot, (1, N_GRP, N_SLAB), 0, N_SLAB)
    sources = jnp.arange(N_SLAB, dtype=jnp.int32)[:, None, None]
    return jnp.where(sources == hottest, CAP, filled)


def draw_send_map(key, part):
    counts = slot_counts(key)
    key = jax.random.fold_in(key, 3)
    picks = jax.random.randint(key, (N_SLAB, N_GRP, N_SLAB, CAP), 0, SLAB_ROWS)
    slot_ids = jnp.arange(CAP, dtype=jnp.int32)
    return jnp.where(slot_ids < counts[..., None], picks, -1).astype(jnp.int32)


def draw_interp_index(key, part):
    counts = slot_counts(key)
    key = jax.random.fold_in(key, 5)
    key_source = jax.random.fold_in(key, 1)
    key_slot = jax.random.fold_in(key, 2)
    shape = (2, N_SLAB, ORI_MAX, NF)
    sources = jax.random.randint(key_source, shape, 0, N_SLAB)
    row_groups = jnp.broadcast_to((jnp.arange(NF, dtype=jnp.int32) // (NF // N_GRP))[None, None, None, :], shape)
    owners = jnp.broadcast_to(jnp.arange(N_SLAB, dtype=jnp.int32)[None, :, None, None], shape)
    limits = counts[sources, row_groups, owners]
    slot_ids = jax.random.randint(key_slot, shape, 0, limits)
    return (sources * CAP + slot_ids).astype(jnp.int32)


def draw_ori_count(key, part):
    key = jax.random.fold_in(key, 7)
    key_len = jax.random.fold_in(key, 1)
    key_top = jax.random.fold_in(key, 2)
    lengths = jax.random.randint(key_len, (N_SLAB,), 1, ORI_MAX + 1)
    longest = jax.random.randint(key_top, (), 0, N_SLAB)
    return jnp.where(jnp.arange(N_SLAB, dtype=jnp.int32) == longest, ORI_MAX, lengths).astype(jnp.int32)


def touch_ends(values, stream_key, smallest, top_value):
    place = [jax.random.randint(jax.random.fold_in(stream_key, axis), (), 0, length) for axis, length in enumerate(values.shape)]
    widest = values.shape.index(max(values.shape))
    beside = place[:widest] + [(place[widest] + 1) % values.shape[widest]] + place[widest + 1:]
    return values.at[tuple(place)].set(smallest).at[tuple(beside)].set(top_value)


def block_scale(own_key, shape, shards, smallest, largest):
    level = 1.0
    for axis_at, parts in shards:
        heights = jax.random.uniform(jax.random.fold_in(jax.random.fold_in(own_key, 6), axis_at), (parts,), jnp.float32, smallest / len(shards), largest / len(shards))
        level = level * jnp.repeat(jnp.exp(heights), shape[axis_at] // parts).reshape((-1,) + (1,) * (len(shape) - 1 - axis_at))
    return level


def gaussian(rng, shape, spread, reach, pieces=(), kind=jnp.bfloat16):
    values = jax.random.normal(rng, shape, jnp.float32) * spread
    if len(pieces) > 0:
        values = block_scale(rng, shape, pieces, -0.22, 0.18) * values
    return jnp.clip(values, min=-reach, max=reach).astype(kind)


def setup_inputs(seed: int = 0) -> dict:
    seeds = jax.random.split(jax.random.key(seed), 9)
    pencils = gaussian(seeds[0], (NF, NF, 2 * NF), 1.0, 6.0, ((0, 8), (1, 4)), jnp.float32)
    send_map = draw_send_map(jax.random.fold_in(seeds[8], 71), 0)
    interp_index = draw_interp_index(jax.random.fold_in(seeds[8], 71), 0)
    interp_frac = jnp.clip(1.0 * jax.random.uniform(seeds[3], (N_SLAB, ORI_MAX, NF), jnp.float32) ** block_scale(seeds[3], (N_SLAB, ORI_MAX, NF), ((0, 8), (2, 4)), -0.2, 0.2), 0.0, 1.0)
    ori_count = draw_ori_count(jax.random.fold_in(seeds[8], 71), 0)
    spectra = gaussian(seeds[5], (PARTICLES, NF, 2 * NF), 1.0, 6.0, ((0, 8), (1, 4)))
    class_ids = touch_ends(jax.random.randint(seeds[6], (PARTICLES,), 0, CLASSES), jax.random.fold_in(seeds[6], 1), 0, CLASSES - 1).astype(jnp.int32)
    ctf_table = jnp.clip(jax.random.uniform(seeds[7], (CLASSES, NF, NF), jnp.float32, -1.0, 1.0) * block_scale(seeds[7], (CLASSES, NF, NF), ((1, 4),), -0.4, 0.0), -1.0, 1.0).astype(jnp.bfloat16)
    return dict(pencils=pencils, send_map=send_map, interp_index=interp_index, interp_frac=interp_frac, ori_count=ori_count, spectra=spectra, class_ids=class_ids, ctf_table=ctf_table)


def phase_factors(first_row, row_total):
    side_ids = jnp.arange(TSIDE, dtype=jnp.int32) - TSIDE // 2
    rows_u = first_row + jnp.arange(row_total, dtype=jnp.int32)
    cols_v = jnp.arange(NF, dtype=jnp.int32)
    turns_u = side_ids[:, None] * rows_u[None, :] % NF
    turns_v = side_ids[:, None] * cols_v[None, :] % NF
    angle_u = -2.0 * math.pi / NF * turns_u.astype(jnp.float32)
    angle_v = -2.0 * math.pi / NF * turns_v.astype(jnp.float32)
    return (jnp.cos(angle_u), jnp.sin(angle_u), jnp.cos(angle_v), jnp.sin(angle_v))

def shift_score(slice_rows, weighted, factors):
    cos_u, sin_u, cos_v, sin_v = factors
    row_total = slice_rows.shape[0]
    cu = cos_u[:, None, :, None]
    su = sin_u[:, None, :, None]
    cv = cos_v[None, :, None, :]
    sv = sin_v[None, :, None, :]
    cosines = (cu * cv - su * sv).reshape(TRANS, row_total, NF)
    sines = (su * cv + cu * sv).reshape(TRANS, row_total, NF)
    real_part = slice_rows[None, :, :NF]
    imag_part = slice_rows[None, :, NF:]
    shifted = jnp.concatenate([real_part * cosines - imag_part * sines, real_part * sines + imag_part * cosines], axis=-1).astype(jnp.bfloat16)
    flat_refs = shifted.reshape(TRANS, -1)
    return lax.dot_general(weighted, flat_refs, (((1,), (1,)), ((), ())), preferred_element_type=jnp.float32) / NF

def reference(pencils, send_map, interp_index, interp_frac, ori_count, spectra, class_ids, ctf_table):
    complex_lines = pencils[..., :NF] + 1j * pencils[..., NF:]
    spectrum = jnp.fft.fft(complex_lines, axis=2) / math.sqrt(NF)
    spectrum = jnp.transpose(spectrum, (2, 0, 1))
    volume_rows = jnp.concatenate([jnp.real(spectrum), jnp.imag(spectrum)], axis=-1).astype(jnp.bfloat16).reshape(NF * NF, 2 * NF)
    slab_starts = jnp.arange(N_SLAB, dtype=jnp.int32) * SLAB_ROWS
    row_group = jnp.arange(NF, dtype=jnp.int32) // (NF // N_GRP)
    factors = phase_factors(0, NF)

    def owner_scores(owner_id):
        slot_map = lax.dynamic_index_in_dim(send_map, owner_id, 2, keepdims=False)
        slot_map = jnp.transpose(slot_map, (1, 0, 2))
        global_rows = (slab_starts[None, :, None] + jnp.maximum(slot_map, 0)).reshape(-1)
        picked = jnp.take(volume_rows, global_rows, axis=0)
        picked = picked * (slot_map >= 0).reshape(-1, 1).astype(jnp.bfloat16)
        tap_index = lax.dynamic_index_in_dim(interp_index, owner_id, 1, keepdims=False)
        weights_tap = lax.dynamic_index_in_dim(interp_frac, owner_id, 0, keepdims=False)[..., None]
        lower_rows = jnp.take(picked, (row_group[None, :] * SLOTS + tap_index[0]).reshape(-1), axis=0).reshape(ORI_MAX, NF, 2 * NF)
        upper_rows = jnp.take(picked, (row_group[None, :] * SLOTS + tap_index[1]).reshape(-1), axis=0).reshape(ORI_MAX, NF, 2 * NF)
        slices = (1.0 - weights_tap) * lower_rows.astype(jnp.float32) + weights_tap * upper_rows.astype(jnp.float32)
        batch = lax.dynamic_slice_in_dim(spectra, owner_id * PART_DEV, PART_DEV, 0)
        classes = lax.dynamic_slice_in_dim(class_ids, owner_id * PART_DEV, PART_DEV, 0)
        ctf_rows = jnp.take(ctf_table, classes, axis=0).astype(jnp.float32)
        weighted = (jnp.concatenate([ctf_rows, ctf_rows], axis=-1) * batch.astype(jnp.float32)).astype(jnp.bfloat16).reshape(PART_DEV, -1)
        live_count = ori_count[owner_id]

        def orient_score(orient):
            result = shift_score(slices[orient], weighted, factors)
            return jnp.where(orient < live_count, result, jnp.zeros_like(result))
        blocks_out = lax.map(orient_score, jnp.arange(ORI_MAX, dtype=jnp.int32))
        return jnp.transpose(blocks_out, (1, 0, 2)).reshape(PART_DEV, ORI_MAX * TRANS)
    result = lax.map(owner_scores, jnp.arange(N_SLAB, dtype=jnp.int32))
    return result.reshape(PARTICLES, ORI_MAX * TRANS)
```

```python
import math

import jax
import jax.numpy as jnp
import numpy as np
from jax import lax
from jax.experimental import pallas as pl
from jax.experimental.pallas import tpu as pltpu
from jax.sharding import PartitionSpec as P

NF = 256
CAP = 16
ORI_MAX = 8
TSIDE = 8
CLASSES = 16
PART_DEV = 8
TRANS = 64


def phase_factors(first_row, row_total):
    side_ids = jnp.arange(TSIDE, dtype=jnp.int32) - TSIDE // 2
    rows_u = first_row + jnp.arange(row_total, dtype=jnp.int32)
    cols_v = jnp.arange(NF, dtype=jnp.int32)
    turns_u = side_ids[:, None] * rows_u[None, :] % NF
    turns_v = side_ids[:, None] * cols_v[None, :] % NF
    angle_u = -2.0 * math.pi / NF * turns_u.astype(jnp.float32)
    angle_v = -2.0 * math.pi / NF * turns_v.astype(jnp.float32)
    return (jnp.cos(angle_u), jnp.sin(angle_u), jnp.cos(angle_v), jnp.sin(angle_v))


def shift_score(slice_rows, weighted, factors):
    cos_u, sin_u, cos_v, sin_v = factors
    row_total = slice_rows.shape[0]
    cu = cos_u[:, None, :, None]
    su = sin_u[:, None, :, None]
    cv = cos_v[None, :, None, :]
    sv = sin_v[None, :, None, :]
    cosines = (cu * cv - su * sv).reshape(TRANS, row_total, NF)
    sines = (su * cv + cu * sv).reshape(TRANS, row_total, NF)
    real_part = slice_rows[None, :, :NF]
    imag_part = slice_rows[None, :, NF:]
    shifted = jnp.concatenate(
        [real_part * cosines - imag_part * sines, real_part * sines + imag_part * cosines], axis=-1
    ).astype(jnp.bfloat16)
    flat_refs = shifted.reshape(TRANS, -1)
    return (
        lax.dot_general(
            weighted, flat_refs, (((1,), (1,)), ((), ())), preferred_element_type=jnp.float32
        )
        / NF
    )


def shards(pencils, send_map, interp_index, interp_frac, ori_count, spectra, class_ids, ctf_table):
    slab_depth = NF // lax.axis_size("slab")
    freq_index = jnp.arange(NF, dtype=jnp.int32)
    phase_turns = freq_index[:, None] * freq_index[None, :] % NF
    angles = 2.0 * math.pi / NF * phase_turns.astype(jnp.float32)
    cosine = jnp.cos(angles)
    sine_table = jnp.sin(angles)
    norm_scale = 1.0 / math.sqrt(NF)
    real_in = pencils[..., :NF]
    imag_in = pencils[..., NF:]
    highest = lax.Precision.HIGHEST
    real_out = (
        jnp.einsum("yxz,zk->kyx", real_in, cosine, precision=highest)
        + jnp.einsum("yxz,zk->kyx", imag_in, sine_table, precision=highest)
    ) * norm_scale
    imag_out = (
        jnp.einsum("yxz,zk->kyx", imag_in, cosine, precision=highest)
        - jnp.einsum("yxz,zk->kyx", real_in, sine_table, precision=highest)
    ) * norm_scale
    planes = jnp.stack([real_out, imag_out], axis=2).astype(jnp.bfloat16)
    slab_planes = lax.all_to_all(planes, "slab", split_axis=0, concat_axis=1, tiled=True)
    gathered = lax.all_gather(slab_planes, "grp", axis=3, tiled=True)
    row_table = gathered.reshape(slab_depth * NF, 2 * NF)
    slot_map = send_map[0, 0]
    picked = jnp.take(row_table, jnp.maximum(slot_map, 0).reshape(-1), axis=0)
    picked = picked * (slot_map >= 0).reshape(-1, 1).astype(jnp.bfloat16)
    outgoing = picked.reshape(slot_map.shape[0], CAP, 2 * NF)
    arrived = lax.all_to_all(outgoing, "slab", split_axis=0, concat_axis=0, tiled=True)
    buffer = arrived.reshape(-1, 2 * NF)
    rows_local = interp_frac.shape[2]
    tap_index = interp_index[:, 0]
    weights_tap = interp_frac[0][..., None]
    lower_rows = jnp.take(buffer, tap_index[0].reshape(-1), axis=0).reshape(
        ORI_MAX, rows_local, 2 * NF
    )
    upper_rows = jnp.take(buffer, tap_index[1].reshape(-1), axis=0).reshape(
        ORI_MAX, rows_local, 2 * NF
    )
    slices = (1.0 - weights_tap) * lower_rows.astype(jnp.float32) + weights_tap * upper_rows.astype(
        jnp.float32
    )
    onehot = (class_ids[:, None] == jnp.arange(CLASSES, dtype=jnp.int32)[None, :]).astype(
        jnp.bfloat16
    )
    ctf_rows = jnp.dot(
        onehot, ctf_table.reshape(CLASSES, -1), preferred_element_type=jnp.float32
    ).reshape(PART_DEV, rows_local, NF)
    weighted = (
        (jnp.concatenate([ctf_rows, ctf_rows], axis=-1) * spectra.astype(jnp.float32))
        .astype(jnp.bfloat16)
        .reshape(PART_DEV, -1)
    )
    first_row = lax.axis_index("grp") * rows_local
    factors = phase_factors(first_row, rows_local)
    live_count = ori_count[0]

    def orient_score(orient):
        result = shift_score(slices[orient], weighted, factors)
        return jnp.where(orient < live_count, result, jnp.zeros_like(result))

    blocks_out = lax.map(orient_score, jnp.arange(ORI_MAX, dtype=jnp.int32))
    partial_scores = jnp.transpose(blocks_out, (1, 0, 2)).reshape(PART_DEV, ORI_MAX * TRANS)
    return lax.psum_scatter(partial_scores, "grp", scatter_dimension=1, tiled=True)


MESH = pl.DeviceIdType.MESH
CAP_FAST = 32


def dft_table():
    turns = np.outer(np.arange(NF), np.arange(NF)) % NF
    angle = 2.0 * np.pi / NF * turns
    cos, sin = np.cos(angle) / math.sqrt(NF), np.sin(angle) / math.sqrt(NF)
    return np.block([[cos, sin], [-sin, cos]]).astype(jnp.bfloat16)


def column_phases():
    side = np.arange(TSIDE) - TSIDE // 2
    angle = 2.0 * np.pi / NF * (np.outer(np.arange(NF), side) % NF)
    cos, sin = np.tile(np.cos(angle), (1, TSIDE)), np.tile(np.sin(angle), (1, TSIDE))
    full = np.block([[cos, -sin], [sin, cos]]).astype(np.float32)
    high = full.astype(jnp.bfloat16)
    low = (full - high.astype(np.float32)).astype(jnp.bfloat16)
    return np.concatenate([high, low], axis=1)


def row_phases():
    side = np.arange(TSIDE) - TSIDE // 2
    angle = 2.0 * np.pi / NF * (np.outer(np.arange(NF), side) % NF)
    cos, sin = np.repeat(np.cos(angle), TSIDE, 1), np.repeat(np.sin(angle), TSIDE, 1)
    return np.concatenate([cos, sin], axis=1).astype(np.float32)


def iota(shape, axis):
    return lax.broadcasted_iota(jnp.int32, shape, axis)


def fused(
    n_slab, n_grp, cap,
    class_ids, ori_count, send_map, index, frac, pencils, dft, spectra, ctf, phase_v, phase_u,
    out, load_out,
    maps, lines, table_w, planes, spec_in, ctf_in, col_ph, row_ph, rank_ref, key_ref, picked, sendbuf,
    recv, weighted, product, part_send, part_recv,
    load_sem, line_sem, map_send, map_recv, row_send, row_recv, sum_send, sum_recv,
):
    s, g = lax.axis_index("slab"), lax.axis_index("grp")
    ky_loc, kx_loc = pencils.shape[0], pencils.shape[1]
    rows_u = spectra.shape[1]
    slots = n_slab * CAP
    chunks = lines.shape[0]
    step = ky_loc // chunks
    peers = [(dg, ds) for dg in range(n_grp) for ds in range(n_slab) if dg + ds > 0]

    def peer(dg, ds):
        return lax.rem(s + ds, n_slab), lax.rem(g + dg, n_grp)

    barrier = pltpu.get_barrier_semaphore()
    for dg, ds in peers:
        pl.semaphore_signal(barrier, inc=1, device_id=peer(dg, ds), device_id_type=MESH)
    loads = [
        pltpu.make_async_copy(a, b, load_sem.at[i])
        for i, (a, b) in enumerate(
            [(dft, table_w), (ctf, ctf_in), (spectra, spec_in), (phase_v, col_ph),
             (phase_u.at[pl.ds(pl.multiple_of(g * rows_u, rows_u), rows_u)], row_ph)]
        )
    ]
    line_loads = [
        pltpu.make_async_copy(pencils.at[pl.ds(c * step, step)], lines.at[c], line_sem.at[c])
        for c in range(chunks)
    ]
    loads[0].start()
    for copy in line_loads:
        copy.start()
    for copy in loads[1:]:
        copy.start()
    own_map = send_map[...]
    maps[s, g] = jnp.concatenate([own_map] * n_slab, axis=1)

    pl.semaphore_wait(barrier, len(peers))

    def map_copy(to, whose):
        return pltpu.make_async_remote_copy(
            src_ref=maps.at[s, g], dst_ref=maps.at[whose[0], whose[1]],
            send_sem=map_send.at[to[0], to[1]], recv_sem=map_recv.at[whose[0], whose[1]],
            device_id=to, device_id_type=MESH)

    for dg, ds in peers:
        map_copy(peer(dg, ds), (s, g)).start()

    loads[0].wait()
    for c in range(chunks):
        line_loads[c].wait()
        block = lines[c].reshape(step * kx_loc, 2 * NF).astype(jnp.bfloat16)
        lanes = lax.dot_general(
            table_w[...], block, (((1,), (1,)), ((), ())), preferred_element_type=jnp.float32
        ).astype(jnp.bfloat16)
        for h in range(step // 2):
            planes[c * (step // 2) + h, :, :128] = lanes[:NF, h * 128:(h + 1) * 128]
            planes[c * (step // 2) + h, :, 128:] = lanes[NF:, h * 128:(h + 1) * 128]

    for dg, ds in peers:
        whose = peer(dg, ds)
        map_copy(whose, whose).wait_recv()

    lane = iota((n_slab, slots), 1)
    rows = jnp.concatenate(
        [sum(jnp.where(lane // CAP == a, maps[a, b], 0) for a in range(n_slab)) for b in range(n_grp)],
        axis=0,
    )
    shift = ky_loc.bit_length() - 1
    used = rows >= 0
    ky = rows & (NF - 1)
    home = jnp.where(used, ky >> shift, -1)
    tri = (iota((slots, slots), 0) < iota((slots, slots), 1)).astype(jnp.float32).astype(jnp.bfloat16)

    def ranks(mask):
        ones = jnp.where(mask, 1.0, 0.0)
        return jnp.dot(ones.astype(jnp.bfloat16), tri, preferred_element_type=jnp.float32), ones

    mine = home == s
    rank, _ = ranks(mine)
    rank = jnp.where(mine, rank, -1.0)
    ky_own = ky & (ky_loc - 1)
    kz = (iota(rows.shape, 1) // CAP) * (NF // n_slab) + (rows >> 8)
    code = (((ky_own >> 1) * NF + kz) * 2 + (ky_own & 1) + 1).astype(jnp.float32)
    for b in range(n_grp):
        rank_ref[b] = rank[b * n_slab:(b + 1) * n_slab]
        key_ref[b] = code[b * n_slab:(b + 1) * n_slab]
    most = jnp.zeros((rows.shape[0], 1), jnp.float32)
    for a in range(n_slab):
        most = jnp.maximum(most, jnp.sum(jnp.where(home == a, 1.0, 0.0), axis=1, keepdims=True))
    load_out[...] = jnp.broadcast_to(jnp.max(most, axis=0, keepdims=True), load_out.shape)

    def row_copy(to, whose):
        return pltpu.make_async_remote_copy(
            src_ref=sendbuf.at[to[1], to[0]],
            dst_ref=recv.at[whose[1], pl.ds(pl.multiple_of(whose[0] * cap, cap), cap)],
            send_sem=row_send.at[to[1], to[0]], recv_sem=row_recv.at[whose[1], whose[0]],
            device_id=to, device_id_type=MESH)

    pairs = ky_loc // 2
    at_once = 256 // cap
    lane256 = iota((256, NF), 1)
    lane128 = iota((256, 128), 1)
    for dg in [1, 2, 3, 0][:n_grp]:
        to_g = lax.rem(g + dg, n_grp)
        for q in range(n_slab // at_once):
            rk = rank_ref[to_g, q * at_once:(q + 1) * at_once]
            cd = key_ref[to_g, q * at_once:(q + 1) * at_once]
            places = iota((at_once, cap, slots), 1).astype(jnp.float32)
            hit = jnp.where(rk[:, None, :] == places, cd[:, None, :], 0.0)
            found = (jnp.sum(hit, axis=2, keepdims=True) - 1.0).reshape(256, 1).astype(jnp.int32)
            odd = (found & 1) == 1
            where_row = found >> 1
            for j in range(pairs):
                picked[:, j * NF:(j + 1) * NF] = jnp.where(
                    where_row - j * NF == lane256, 1.0, 0.0).astype(jnp.bfloat16)
            got = jnp.dot(picked[...], planes[...].reshape(pairs * NF, 256),
                          preferred_element_type=jnp.float32)
            a, b = got[:, :128], got[:, 128:]
            row = jnp.where(lane128 < 64, jnp.where(odd, pltpu.roll(a, 64, 1), a),
                            jnp.where(odd, b, pltpu.roll(b, 64, 1)))
            sendbuf[to_g, q * at_once:(q + 1) * at_once] = row.astype(jnp.bfloat16).reshape(at_once, cap, 128)
        for ds in range(n_slab):
            if dg + ds > 0:
                row_copy(peer(dg, ds), (s, g)).start()
    recv[g, pl.ds(pl.multiple_of(s * cap, cap), cap)] = sendbuf[g, s]

    for copy in loads[1:]:
        copy.wait()
    for p in range(PART_DEV):
        ctf_rows = ctf_in[class_ids[p]].astype(jnp.float32)
        for part in range(2):
            weighted[p, :, part * NF:(part + 1) * NF] = (
                ctf_rows * spec_in[p, :, part * NF:(part + 1) * NF].astype(jnp.float32)
            ).astype(jnp.bfloat16)

    own = jnp.sum(jnp.where(lane // CAP == iota((n_slab, slots), 0), maps_row(maps, s, g, n_slab), 0),
                  axis=0, keepdims=True)
    own_home = jnp.where(own >= 0, (own & (NF - 1)) >> shift, -1)
    from_a = own_home == iota((n_slab, slots), 0)
    own_rank, ones = ranks(from_a)
    base = (iota((n_slab, slots), 0) * cap).astype(jnp.float32)
    place = jnp.sum(ones * (own_rank + base + 1.0), axis=0, keepdims=True) - 1.0
    spread = jnp.where(place == iota((n_slab * cap, slots), 0).astype(jnp.float32), 1.0, 0.0).astype(jnp.bfloat16)

    for dg, ds in peers:
        whose = peer(dg, ds)
        row_copy(whose, whose).wait_recv()
    lists = [
        lax.dot_general(spread, recv[b], (((0,), (0,)), ((), ())), preferred_element_type=jnp.float32)
        for b in range(n_grp)
    ]
    lane_s = iota((slots, 128), 1)
    real, imag = [], []
    for b in range(0, n_grp, 2):
        x, y = lists[b], lists[b + 1]
        real.append(jnp.where(lane_s < 64, x, pltpu.roll(y, 64, 1)))
        imag.append(jnp.where(lane_s < 64, pltpu.roll(x, 64, 1), y))
    received = jnp.concatenate(real + imag, axis=1).astype(jnp.bfloat16)
    received = jnp.concatenate([received, received], axis=0)

    def sum_copy(to_g, whose_g):
        return pltpu.make_async_remote_copy(
            src_ref=part_send.at[to_g], dst_ref=part_recv.at[whose_g],
            send_sem=sum_send.at[to_g], recv_sem=sum_recv.at[whose_g],
            device_id=(s, to_g), device_id_type=MESH)

    slot_id = iota((slots, rows_u), 0)
    live = ori_count[0]
    lane_p = iota((PART_DEV, 128), 1)
    for dg in [1, 2, 3, 0][:n_grp]:
        to_g = lax.rem(g + dg, n_grp)
        folded = []
        for half in range(2):
            o = to_g * 2 + half
            i0 = index[0, pl.ds(o, 1), :]
            i1 = index[1, pl.ds(o, 1), :]
            w = frac[pl.ds(o, 1), :]
            taps = jnp.where(slot_id == i0, 1.0 - w, 0.0) + jnp.where(slot_id == i1, w, 0.0)
            high = taps.astype(jnp.bfloat16)
            low = (taps - high.astype(jnp.float32)).astype(jnp.bfloat16)
            rows_o = lax.dot_general(
                jnp.concatenate([high, low], axis=0), received, (((0,), (0,)), ((), ())),
                preferred_element_type=jnp.float32)
            sr, si = rows_o[:, :NF], rows_o[:, NF:]
            for p in range(PART_DEV):
                wr = weighted[p, :, :NF].astype(jnp.float32)
                wi = weighted[p, :, NF:].astype(jnp.float32)
                product[p * rows_u:(p + 1) * rows_u, :NF] = (wr * sr + wi * si).astype(jnp.bfloat16)
                product[p * rows_u:(p + 1) * rows_u, NF:] = (wr * si - wi * sr).astype(jnp.bfloat16)
            z = jnp.dot(product[...], col_ph[...], preferred_element_type=jnp.float32)
            z = (z[:, :128] + z[:, 128:]).reshape(PART_DEV, rows_u, 128)
            t = jnp.sum(z * row_ph[...][None], axis=1)
            t = (t + pltpu.roll(t, 64, 1)) * (1.0 / NF)
            folded.append(jnp.where(o < live, t, 0.0))
        block = jnp.where(lane_p < 64, folded[0], folded[1])
        if dg > 0:
            part_send[to_g] = block
            sum_copy(to_g, g).start()
        else:
            total = block
    for dg in range(1, n_grp):
        from_g = lax.rem(g + dg, n_grp)
        sum_copy(from_g, from_g).wait_recv()
        total += part_recv[from_g]
    out[...] = total

    for dg, ds in peers:
        to = peer(dg, ds)
        map_copy(to, (s, g)).wait_send()
        row_copy(to, (s, g)).wait_send()
    for dg in range(1, n_grp):
        sum_copy(lax.rem(g + dg, n_grp), g).wait_send()


def maps_row(maps, s, g, n_slab):
    return jnp.concatenate([maps[a, g, pl.ds(s, 1), :] for a in range(n_slab)], axis=0)


def run_fused(n_slab, n_grp, cap, collective_id, args):
    pencils, send_map, index, frac, ori_count, spectra, class_ids, ctf = args
    ky_loc, kx_loc = pencils.shape[:2]
    rows_u = spectra.shape[1]
    slots = n_slab * CAP
    chunks = ky_loc // 4
    vmem, smem, hbm = (pl.BlockSpec(memory_space=m) for m in (pltpu.VMEM, pltpu.SMEM, pl.ANY))
    dma = pltpu.SemaphoreType.DMA
    return pl.pallas_call(
        lambda *refs: fused(n_slab, n_grp, cap, *refs),
        out_shape=[
            jax.ShapeDtypeStruct((PART_DEV, ORI_MAX * TRANS // n_grp), jnp.float32),
            jax.ShapeDtypeStruct((8, 128), jnp.float32),
        ],
        in_specs=[smem, smem, vmem, vmem, vmem, hbm, hbm, hbm, hbm, hbm, hbm],
        out_specs=[vmem, vmem],
        scratch_shapes=[
            pltpu.VMEM((n_slab, n_grp, n_slab, slots), jnp.int32),
            pltpu.VMEM((chunks, 4, kx_loc, 2 * NF), jnp.float32),
            pltpu.VMEM((2 * NF, 2 * NF), jnp.bfloat16),
            pltpu.VMEM((ky_loc // 2, NF, 256), jnp.bfloat16),
            pltpu.VMEM(spectra.shape, jnp.bfloat16),
            pltpu.VMEM(ctf.shape, jnp.bfloat16),
            pltpu.VMEM((2 * NF, 256), jnp.bfloat16),
            pltpu.VMEM((rows_u, 128), jnp.float32),
            pltpu.VMEM((n_grp, n_slab, slots), jnp.float32),
            pltpu.VMEM((n_grp, n_slab, slots), jnp.float32),
            pltpu.VMEM((256, ky_loc // 2 * NF), jnp.bfloat16),
            pltpu.VMEM((n_grp, n_slab, cap, 128), jnp.bfloat16),
            pltpu.VMEM((n_grp, n_slab * cap, 128), jnp.bfloat16),
            pltpu.VMEM(spectra.shape, jnp.bfloat16),
            pltpu.VMEM((PART_DEV * rows_u, 2 * NF), jnp.bfloat16),
            pltpu.VMEM((n_grp, PART_DEV, 128), jnp.float32),
            pltpu.VMEM((n_grp, PART_DEV, 128), jnp.float32),
            dma((5,)),
            dma((chunks,)),
            dma((n_slab, n_grp)),
            dma((n_slab, n_grp)),
            dma((n_grp, n_slab)),
            dma((n_grp, n_slab)),
            dma((n_grp,)),
            dma((n_grp,)),
        ],
        compiler_params=pltpu.CompilerParams(
            collective_id=collective_id, has_side_effects=True, vmem_limit_bytes=48 * 2**20),
    )(
        class_ids, ori_count, send_map[0, 0], index[:, 0], frac[0], pencils, jnp.asarray(dft_table()),
        spectra, ctf, jnp.asarray(column_phases()), jnp.asarray(row_phases()),
    )


def listed(n_slab, n_grp, *args):
    scores, load = run_fused(n_slab, n_grp, CAP_FAST, 1, args)
    return lax.cond(
        load[0, 0] > CAP_FAST,
        lambda: run_fused(n_slab, n_grp, n_slab * CAP, 2, args)[0],
        lambda: scores,
    )


def solution(mesh):
    n_slab, n_grp = mesh.shape["slab"], mesh.shape["grp"]

    def body(*args):
        if n_slab * CAP == 128 and n_grp == 4:
            return listed(n_slab, n_grp, *args)
        return shards(*args)

    return jax.shard_map(
        body,
        mesh=mesh,
        in_specs=(
            P("slab", "grp", None),
            P("slab", "grp", None, None),
            P(None, "slab", None, "grp"),
            P("slab", None, "grp"),
            P("slab"),
            P("slab", "grp", None),
            P("slab"),
            P(None, "grp", None),
        ),
        out_specs=P("slab", "grp"),
        check_vma=False,
    )
```

```python
import math

import jax
import jax.numpy as jnp
import numpy as np
from jax import lax
from jax.experimental import pallas as pl
from jax.experimental.pallas import tpu as pltpu
from jax.sharding import PartitionSpec as P

NF = 256
CAP = 16
ORI_MAX = 8
TSIDE = 8
CLASSES = 16
PART_DEV = 8
TRANS = 64


def phase_factors(first_row, row_total):
    side_ids = jnp.arange(TSIDE, dtype=jnp.int32) - TSIDE // 2
    rows_u = first_row + jnp.arange(row_total, dtype=jnp.int32)
    cols_v = jnp.arange(NF, dtype=jnp.int32)
    turns_u = side_ids[:, None] * rows_u[None, :] % NF
    turns_v = side_ids[:, None] * cols_v[None, :] % NF
    angle_u = -2.0 * math.pi / NF * turns_u.astype(jnp.float32)
    angle_v = -2.0 * math.pi / NF * turns_v.astype(jnp.float32)
    return (jnp.cos(angle_u), jnp.sin(angle_u), jnp.cos(angle_v), jnp.sin(angle_v))


def shift_score(slice_rows, weighted, factors):
    cos_u, sin_u, cos_v, sin_v = factors
    row_total = slice_rows.shape[0]
    cu = cos_u[:, None, :, None]
    su = sin_u[:, None, :, None]
    cv = cos_v[None, :, None, :]
    sv = sin_v[None, :, None, :]
    cosines = (cu * cv - su * sv).reshape(TRANS, row_total, NF)
    sines = (su * cv + cu * sv).reshape(TRANS, row_total, NF)
    real_part = slice_rows[None, :, :NF]
    imag_part = slice_rows[None, :, NF:]
    shifted = jnp.concatenate(
        [real_part * cosines - imag_part * sines, real_part * sines + imag_part * cosines], axis=-1
    ).astype(jnp.bfloat16)
    flat_refs = shifted.reshape(TRANS, -1)
    return (
        lax.dot_general(
            weighted, flat_refs, (((1,), (1,)), ((), ())), preferred_element_type=jnp.float32
        )
        / NF
    )


def shards(pencils, send_map, interp_index, interp_frac, ori_count, spectra, class_ids, ctf_table):
    slab_depth = NF // lax.axis_size("slab")
    freq_index = jnp.arange(NF, dtype=jnp.int32)
    phase_turns = freq_index[:, None] * freq_index[None, :] % NF
    angles = 2.0 * math.pi / NF * phase_turns.astype(jnp.float32)
    cosine = jnp.cos(angles)
    sine_table = jnp.sin(angles)
    norm_scale = 1.0 / math.sqrt(NF)
    real_in = pencils[..., :NF]
    imag_in = pencils[..., NF:]
    highest = lax.Precision.HIGHEST
    real_out = (
        jnp.einsum("yxz,zk->kyx", real_in, cosine, precision=highest)
        + jnp.einsum("yxz,zk->kyx", imag_in, sine_table, precision=highest)
    ) * norm_scale
    imag_out = (
        jnp.einsum("yxz,zk->kyx", imag_in, cosine, precision=highest)
        - jnp.einsum("yxz,zk->kyx", real_in, sine_table, precision=highest)
    ) * norm_scale
    planes = jnp.stack([real_out, imag_out], axis=2).astype(jnp.bfloat16)
    slab_planes = lax.all_to_all(planes, "slab", split_axis=0, concat_axis=1, tiled=True)
    gathered = lax.all_gather(slab_planes, "grp", axis=3, tiled=True)
    row_table = gathered.reshape(slab_depth * NF, 2 * NF)
    slot_map = send_map[0, 0]
    picked = jnp.take(row_table, jnp.maximum(slot_map, 0).reshape(-1), axis=0)
    picked = picked * (slot_map >= 0).reshape(-1, 1).astype(jnp.bfloat16)
    outgoing = picked.reshape(slot_map.shape[0], CAP, 2 * NF)
    arrived = lax.all_to_all(outgoing, "slab", split_axis=0, concat_axis=0, tiled=True)
    buffer = arrived.reshape(-1, 2 * NF)
    rows_local = interp_frac.shape[2]
    tap_index = interp_index[:, 0]
    weights_tap = interp_frac[0][..., None]
    lower_rows = jnp.take(buffer, tap_index[0].reshape(-1), axis=0).reshape(
        ORI_MAX, rows_local, 2 * NF
    )
    upper_rows = jnp.take(buffer, tap_index[1].reshape(-1), axis=0).reshape(
        ORI_MAX, rows_local, 2 * NF
    )
    slices = (1.0 - weights_tap) * lower_rows.astype(jnp.float32) + weights_tap * upper_rows.astype(
        jnp.float32
    )
    onehot = (class_ids[:, None] == jnp.arange(CLASSES, dtype=jnp.int32)[None, :]).astype(
        jnp.bfloat16
    )
    ctf_rows = jnp.dot(
        onehot, ctf_table.reshape(CLASSES, -1), preferred_element_type=jnp.float32
    ).reshape(PART_DEV, rows_local, NF)
    weighted = (
        (jnp.concatenate([ctf_rows, ctf_rows], axis=-1) * spectra.astype(jnp.float32))
        .astype(jnp.bfloat16)
        .reshape(PART_DEV, -1)
    )
    first_row = lax.axis_index("grp") * rows_local
    factors = phase_factors(first_row, rows_local)
    live_count = ori_count[0]

    def orient_score(orient):
        result = shift_score(slices[orient], weighted, factors)
        return jnp.where(orient < live_count, result, jnp.zeros_like(result))

    blocks_out = lax.map(orient_score, jnp.arange(ORI_MAX, dtype=jnp.int32))
    partial_scores = jnp.transpose(blocks_out, (1, 0, 2)).reshape(PART_DEV, ORI_MAX * TRANS)
    return lax.psum_scatter(partial_scores, "grp", scatter_dimension=1, tiled=True)


MESH = pl.DeviceIdType.MESH
CAP_FAST = 32


def dft_table():
    turns = np.outer(np.arange(NF), np.arange(NF)) % NF
    angle = 2.0 * np.pi / NF * turns
    cos, sin = np.cos(angle) / math.sqrt(NF), np.sin(angle) / math.sqrt(NF)
    return np.block([[cos, sin], [-sin, cos]]).astype(jnp.bfloat16)


def column_phases():
    side = np.arange(TSIDE) - TSIDE // 2
    angle = 2.0 * np.pi / NF * (np.outer(np.arange(NF), side) % NF)
    cos, sin = np.tile(np.cos(angle), (1, TSIDE)), np.tile(np.sin(angle), (1, TSIDE))
    full = np.block([[cos, -sin], [sin, cos]]).astype(np.float32)
    high = full.astype(jnp.bfloat16)
    low = (full - high.astype(np.float32)).astype(jnp.bfloat16)
    return np.concatenate([high, low], axis=1)


def row_phases():
    side = np.arange(TSIDE) - TSIDE // 2
    angle = 2.0 * np.pi / NF * (np.outer(np.arange(NF), side) % NF)
    cos, sin = np.repeat(np.cos(angle), TSIDE, 1), np.repeat(np.sin(angle), TSIDE, 1)
    return np.concatenate([cos, sin], axis=1).astype(np.float32)


def iota(shape, axis):
    return lax.broadcasted_iota(jnp.int32, shape, axis)


def fused(
    n_slab, n_grp, cap,
    class_ids, ori_count, send_map, index, frac, pencils, dft, spectra, ctf, phase_v, phase_u,
    out, load_out,
    maps, lines, table_w, planes, spec_in, ctf_in, col_ph, row_ph, rank_ref, key_ref, picked, sendbuf,
    recv, weighted, product, part_send, part_recv,
    load_sem, line_sem, map_send, map_recv, row_send, row_recv, sum_send, sum_recv,
):
    s, g = lax.axis_index("slab"), lax.axis_index("grp")
    ky_loc, kx_loc = pencils.shape[0], pencils.shape[1]
    rows_u = spectra.shape[1]
    slots = n_slab * CAP
    chunks = lines.shape[0]
    step = ky_loc // chunks
    peers = [(dg, ds) for dg in range(n_grp) for ds in range(n_slab) if dg + ds > 0]

    def peer(dg, ds):
        return lax.rem(s + ds, n_slab), lax.rem(g + dg, n_grp)

    barrier = pltpu.get_barrier_semaphore()
    for dg, ds in peers:
        pl.semaphore_signal(barrier, inc=1, device_id=peer(dg, ds), device_id_type=MESH)
    loads = [
        pltpu.make_async_copy(a, b, load_sem.at[i])
        for i, (a, b) in enumerate(
            [(dft, table_w), (ctf, ctf_in), (spectra, spec_in), (phase_v, col_ph),
             (phase_u.at[pl.ds(pl.multiple_of(g * rows_u, rows_u), rows_u)], row_ph)]
        )
    ]

    def line_load(c):
        return pltpu.make_async_copy(pencils.at[pl.ds(c * step, step)], lines.at[c], line_sem.at[c])

    loads[0].start()
    for c in range(chunks):
        line_load(c).start()
    for copy in loads[1:]:
        copy.start()
    own_map = send_map[...]
    maps[s, g] = jnp.concatenate([own_map] * n_slab, axis=1)

    def transform(c, carry):
        line_load(c).wait()
        block = lines[c].reshape(step * kx_loc, 2 * NF).astype(jnp.bfloat16)
        lanes = lax.dot_general(
            table_w[...], block, (((1,), (1,)), ((), ())), preferred_element_type=jnp.float32
        ).astype(jnp.bfloat16)
        for h in range(step // 2):
            planes[c * (step // 2) + h, :, :128] = lanes[:NF, h * 128:(h + 1) * 128]
            planes[c * (step // 2) + h, :, 128:] = lanes[NF:, h * 128:(h + 1) * 128]
        return carry

    loads[0].wait()
    lax.fori_loop(0, chunks // 2, transform, 0)
    pl.semaphore_wait(barrier, len(peers))

    def map_copy(to, whose):
        return pltpu.make_async_remote_copy(
            src_ref=maps.at[s, g], dst_ref=maps.at[whose[0], whose[1]],
            send_sem=map_send.at[to[0], to[1]], recv_sem=map_recv.at[whose[0], whose[1]],
            device_id=to, device_id_type=MESH)

    for dg, ds in peers:
        map_copy(peer(dg, ds), (s, g)).start()

    lax.fori_loop(chunks // 2, chunks, transform, 0)

    for dg, ds in peers:
        whose = peer(dg, ds)
        map_copy(whose, whose).wait_recv()

    lane = iota((n_slab, slots), 1)
    rows = jnp.concatenate(
        [sum(jnp.where(lane // CAP == a, maps[a, b], 0) for a in range(n_slab)) for b in range(n_grp)],
        axis=0,
    )
    shift = ky_loc.bit_length() - 1
    used = rows >= 0
    ky = rows & (NF - 1)
    home = jnp.where(used, ky >> shift, -1)
    tri = (iota((slots, slots), 0) < iota((slots, slots), 1)).astype(jnp.float32).astype(jnp.bfloat16)

    def ranks(mask):
        ones = jnp.where(mask, 1.0, 0.0)
        return jnp.dot(ones.astype(jnp.bfloat16), tri, preferred_element_type=jnp.float32), ones

    mine = home == s
    rank, _ = ranks(mine)
    rank = jnp.where(mine, rank, -1.0)
    ky_own = ky & (ky_loc - 1)
    kz = (iota(rows.shape, 1) // CAP) * (NF // n_slab) + (rows >> 8)
    code = (((ky_own >> 1) * NF + kz) * 2 + (ky_own & 1) + 1).astype(jnp.float32)
    for b in range(n_grp):
        rank_ref[b] = rank[b * n_slab:(b + 1) * n_slab]
        key_ref[b] = code[b * n_slab:(b + 1) * n_slab]
    most = jnp.zeros((rows.shape[0], 1), jnp.float32)
    for a in range(n_slab):
        most = jnp.maximum(most, jnp.sum(jnp.where(home == a, 1.0, 0.0), axis=1, keepdims=True))
    load_out[0] = (jnp.max(most) > cap).astype(jnp.int32)

    def row_copy(to, whose):
        return pltpu.make_async_remote_copy(
            src_ref=sendbuf.at[to[1], to[0]],
            dst_ref=recv.at[whose[1], pl.ds(pl.multiple_of(whose[0] * cap, cap), cap)],
            send_sem=row_send.at[to[1], to[0]], recv_sem=row_recv.at[whose[1], whose[0]],
            device_id=to, device_id_type=MESH)

    pairs = ky_loc // 2
    at_once = 256 // cap
    lane256 = iota((256, NF), 1)
    lane128 = iota((256, 128), 1)

    def pick(i, carry):
        to_g = lax.rem(g + i + 1, n_grp)
        for q in range(n_slab // at_once):
            rk = rank_ref[to_g, q * at_once:(q + 1) * at_once]
            cd = key_ref[to_g, q * at_once:(q + 1) * at_once]
            places = iota((at_once, cap, slots), 1).astype(jnp.float32)
            hit = jnp.where(rk[:, None, :] == places, cd[:, None, :], 0.0)
            found = (jnp.sum(hit, axis=2, keepdims=True) - 1.0).reshape(256, 1).astype(jnp.int32)
            odd = (found & 1) == 1
            pair = jnp.broadcast_to((found >> (NF.bit_length())).astype(jnp.float32), (256, NF)).astype(jnp.bfloat16)
            plane_hit = jnp.where(((found >> 1) & (NF - 1)) == lane256, 1.0, 0.0).astype(jnp.bfloat16)
            for j in range(pairs):
                picked[:, j * NF:(j + 1) * NF] = jnp.where(
                    pair == jnp.bfloat16(j), plane_hit, jnp.bfloat16(0))
            got = jnp.dot(picked[...], planes[...].reshape(pairs * NF, 256),
                          preferred_element_type=jnp.float32)
            a, b = got[:, :128], got[:, 128:]
            row = jnp.where(lane128 < 64, jnp.where(odd, pltpu.roll(a, 64, 1), a),
                            jnp.where(odd, b, pltpu.roll(b, 64, 1)))
            sendbuf[to_g, q * at_once:(q + 1) * at_once] = row.astype(jnp.bfloat16).reshape(at_once, cap, 128)
        for ds in range(n_slab):
            to = (lax.rem(s + ds, n_slab), to_g)
            if ds > 0:
                row_copy(to, (s, g)).start()
            else:
                @pl.when(i < n_grp - 1)
                def _():
                    row_copy(to, (s, g)).start()
        return carry

    lax.fori_loop(0, n_grp, pick, 0)
    recv[g, pl.ds(pl.multiple_of(s * cap, cap), cap)] = sendbuf[g, s]

    for copy in loads[1:]:
        copy.wait()
    for p in range(PART_DEV):
        ctf_rows = ctf_in[class_ids[p]].astype(jnp.float32)
        for part in range(2):
            weighted[p, :, part * NF:(part + 1) * NF] = (
                ctf_rows * spec_in[p, :, part * NF:(part + 1) * NF].astype(jnp.float32)
            ).astype(jnp.bfloat16)

    own = jnp.sum(jnp.where(lane // CAP == iota((n_slab, slots), 0), maps_row(maps, s, g, n_slab), 0),
                  axis=0, keepdims=True)
    own_home = jnp.where(own >= 0, (own & (NF - 1)) >> shift, -1)
    from_a = own_home == iota((n_slab, slots), 0)
    own_rank, ones = ranks(from_a)
    base = (iota((n_slab, slots), 0) * cap).astype(jnp.float32)
    place = jnp.sum(ones * (own_rank + base + 1.0), axis=0, keepdims=True) - 1.0
    spread = jnp.where(place == iota((n_slab * cap, slots), 0).astype(jnp.float32), 1.0, 0.0).astype(jnp.bfloat16)

    for dg, ds in peers:
        map_copy(peer(dg, ds), (s, g)).wait_send()
    for dg, ds in peers:
        whose = peer(dg, ds)
        row_copy(whose, whose).wait_recv()
    lists = [
        lax.dot_general(spread, recv[b], (((0,), (0,)), ((), ())), preferred_element_type=jnp.float32)
        for b in range(n_grp)
    ]
    lane_s = iota((slots, 128), 1)
    real, imag = [], []
    for b in range(0, n_grp, 2):
        x, y = lists[b], lists[b + 1]
        real.append(jnp.where(lane_s < 64, x, pltpu.roll(y, 64, 1)))
        imag.append(jnp.where(lane_s < 64, pltpu.roll(x, 64, 1), y))
    received = jnp.concatenate(real + imag, axis=1).astype(jnp.bfloat16)
    received = jnp.concatenate([received, received], axis=0)

    def sum_copy(to_g, whose_g):
        return pltpu.make_async_remote_copy(
            src_ref=part_send.at[to_g], dst_ref=part_recv.at[whose_g],
            send_sem=sum_send.at[to_g], recv_sem=sum_recv.at[whose_g],
            device_id=(s, to_g), device_id_type=MESH)

    slot_id = iota((slots, rows_u), 0)
    live = ori_count[0]
    lane_p = iota((PART_DEV, 128), 1)

    def score(i, carry):
        to_g = lax.rem(g + i + 1, n_grp)
        folded = []
        for half in range(2):
            o = to_g * 2 + half
            i0 = index[0, pl.ds(o, 1), :]
            i1 = index[1, pl.ds(o, 1), :]
            w = frac[pl.ds(o, 1), :]
            taps = jnp.where(slot_id == i0, 1.0 - w, 0.0) + jnp.where(slot_id == i1, w, 0.0)
            high = taps.astype(jnp.bfloat16)
            low = (taps - high.astype(jnp.float32)).astype(jnp.bfloat16)
            rows_o = lax.dot_general(
                jnp.concatenate([high, low], axis=0), received, (((0,), (0,)), ((), ())),
                preferred_element_type=jnp.float32)
            sr, si = rows_o[:, :NF], rows_o[:, NF:]
            for p in range(PART_DEV):
                wr = weighted[p, :, :NF].astype(jnp.float32)
                wi = weighted[p, :, NF:].astype(jnp.float32)
                product[p * rows_u:(p + 1) * rows_u, :NF] = (wr * sr + wi * si).astype(jnp.bfloat16)
                product[p * rows_u:(p + 1) * rows_u, NF:] = (wr * si - wi * sr).astype(jnp.bfloat16)
            z = jnp.dot(product[...], col_ph[...], preferred_element_type=jnp.float32)
            z = (z[:, :128] + z[:, 128:]).reshape(PART_DEV, rows_u, 128)
            t = jnp.sum(z * row_ph[...][None], axis=1)
            t = (t + pltpu.roll(t, 64, 1)) * (1.0 / NF)
            folded.append(jnp.where(o < live, t, 0.0))
        block = jnp.where(lane_p < 64, folded[0], folded[1])
        part_send[to_g] = block

        @pl.when(i < n_grp - 1)
        def _():
            sum_copy(to_g, g).start()

        return carry

    lax.fori_loop(0, n_grp, score, 0)
    for dg, ds in peers:
        row_copy(peer(dg, ds), (s, g)).wait_send()
    total = part_send[g]
    for dg in range(1, n_grp):
        from_g = lax.rem(g + dg, n_grp)
        sum_copy(from_g, from_g).wait_recv()
        total += part_recv[from_g]
    out[...] = total
    for dg in range(1, n_grp):
        sum_copy(lax.rem(g + dg, n_grp), g).wait_send()


def maps_row(maps, s, g, n_slab):
    return jnp.concatenate([maps[a, g, pl.ds(s, 1), :] for a in range(n_slab)], axis=0)


def run_fused(n_slab, n_grp, cap, collective_id, args):
    pencils, send_map, index, frac, ori_count, spectra, class_ids, ctf = args
    ky_loc, kx_loc = pencils.shape[:2]
    rows_u = spectra.shape[1]
    slots = n_slab * CAP
    chunks = ky_loc // 4
    vmem, smem, hbm = (pl.BlockSpec(memory_space=m) for m in (pltpu.VMEM, pltpu.SMEM, pl.ANY))
    dma = pltpu.SemaphoreType.DMA
    return pl.pallas_call(
        lambda *refs: fused(n_slab, n_grp, cap, *refs),
        out_shape=[
            jax.ShapeDtypeStruct((PART_DEV, ORI_MAX * TRANS // n_grp), jnp.float32),
            jax.ShapeDtypeStruct((1,), jnp.int32),
        ],
        in_specs=[smem, smem, vmem, vmem, vmem, hbm, hbm, hbm, hbm, hbm, hbm],
        out_specs=[vmem, smem],
        scratch_shapes=[
            pltpu.VMEM((n_slab, n_grp, n_slab, slots), jnp.int32),
            pltpu.VMEM((chunks, 4, kx_loc, 2 * NF), jnp.float32),
            pltpu.VMEM((2 * NF, 2 * NF), jnp.bfloat16),
            pltpu.VMEM((ky_loc // 2, NF, 256), jnp.bfloat16),
            pltpu.VMEM(spectra.shape, jnp.bfloat16),
            pltpu.VMEM(ctf.shape, jnp.bfloat16),
            pltpu.VMEM((2 * NF, 256), jnp.bfloat16),
            pltpu.VMEM((rows_u, 128), jnp.float32),
            pltpu.VMEM((n_grp, n_slab, slots), jnp.float32),
            pltpu.VMEM((n_grp, n_slab, slots), jnp.float32),
            pltpu.VMEM((256, ky_loc // 2 * NF), jnp.bfloat16),
            pltpu.VMEM((n_grp, n_slab, cap, 128), jnp.bfloat16),
            pltpu.VMEM((n_grp, n_slab * cap, 128), jnp.bfloat16),
            pltpu.VMEM(spectra.shape, jnp.bfloat16),
            pltpu.VMEM((PART_DEV * rows_u, 2 * NF), jnp.bfloat16),
            pltpu.VMEM((n_grp, PART_DEV, 128), jnp.float32),
            pltpu.VMEM((n_grp, PART_DEV, 128), jnp.float32),
            dma((5,)),
            dma((chunks,)),
            dma((n_slab, n_grp)),
            dma((n_slab, n_grp)),
            dma((n_grp, n_slab)),
            dma((n_grp, n_slab)),
            dma((n_grp,)),
            dma((n_grp,)),
        ],
        compiler_params=pltpu.CompilerParams(
            collective_id=collective_id, has_side_effects=True, vmem_limit_bytes=60 * 2**20),
    )(
        class_ids, ori_count, send_map[0, 0], index[:, 0], frac[0], pencils, jnp.asarray(dft_table()),
        spectra, ctf, jnp.asarray(column_phases()), jnp.asarray(row_phases()),
    )


def listed(n_slab, n_grp, *args):
    scores, load = run_fused(n_slab, n_grp, CAP_FAST, 1, args)
    return lax.cond(
        load.reshape(()) > 0,
        lambda: run_fused(n_slab, n_grp, n_slab * CAP, 2, args)[0],
        lambda: scores,
    )


def solution(mesh):
    n_slab, n_grp = mesh.shape["slab"], mesh.shape["grp"]

    def body(*args):
        if n_slab * CAP == 128 and n_grp == 4:
            return listed(n_slab, n_grp, *args)
        return shards(*args)

    return jax.shard_map(
        body,
        mesh=mesh,
        in_specs=(
            P("slab", "grp", None),
            P("slab", "grp", None, None),
            P(None, "slab", None, "grp"),
            P("slab", None, "grp"),
            P("slab"),
            P("slab", "grp", None),
            P("slab"),
            P(None, "grp", None),
        ),
        out_specs=P("slab", "grp"),
        check_vma=False,
    )
```

```python
import math

import jax
import jax.numpy as jnp
import numpy as np
from jax import lax
from jax.experimental import pallas as pl
from jax.experimental.pallas import tpu as pltpu
from jax.sharding import PartitionSpec as P

NF = 256
CAP = 16
ORI_MAX = 8
TSIDE = 8
CLASSES = 16
PART_DEV = 8
TRANS = 64


def phase_factors(first_row, row_total):
    side_ids = jnp.arange(TSIDE, dtype=jnp.int32) - TSIDE // 2
    rows_u = first_row + jnp.arange(row_total, dtype=jnp.int32)
    cols_v = jnp.arange(NF, dtype=jnp.int32)
    turns_u = side_ids[:, None] * rows_u[None, :] % NF
    turns_v = side_ids[:, None] * cols_v[None, :] % NF
    angle_u = -2.0 * math.pi / NF * turns_u.astype(jnp.float32)
    angle_v = -2.0 * math.pi / NF * turns_v.astype(jnp.float32)
    return (jnp.cos(angle_u), jnp.sin(angle_u), jnp.cos(angle_v), jnp.sin(angle_v))


def shift_score(slice_rows, weighted, factors):
    cos_u, sin_u, cos_v, sin_v = factors
    row_total = slice_rows.shape[0]
    cu = cos_u[:, None, :, None]
    su = sin_u[:, None, :, None]
    cv = cos_v[None, :, None, :]
    sv = sin_v[None, :, None, :]
    cosines = (cu * cv - su * sv).reshape(TRANS, row_total, NF)
    sines = (su * cv + cu * sv).reshape(TRANS, row_total, NF)
    real_part = slice_rows[None, :, :NF]
    imag_part = slice_rows[None, :, NF:]
    shifted = jnp.concatenate(
        [real_part * cosines - imag_part * sines, real_part * sines + imag_part * cosines], axis=-1
    ).astype(jnp.bfloat16)
    flat_refs = shifted.reshape(TRANS, -1)
    return (
        lax.dot_general(
            weighted, flat_refs, (((1,), (1,)), ((), ())), preferred_element_type=jnp.float32
        )
        / NF
    )


def shards(pencils, send_map, interp_index, interp_frac, ori_count, spectra, class_ids, ctf_table):
    slab_depth = NF // lax.axis_size("slab")
    freq_index = jnp.arange(NF, dtype=jnp.int32)
    phase_turns = freq_index[:, None] * freq_index[None, :] % NF
    angles = 2.0 * math.pi / NF * phase_turns.astype(jnp.float32)
    cosine = jnp.cos(angles)
    sine_table = jnp.sin(angles)
    norm_scale = 1.0 / math.sqrt(NF)
    real_in = pencils[..., :NF]
    imag_in = pencils[..., NF:]
    highest = lax.Precision.HIGHEST
    real_out = (
        jnp.einsum("yxz,zk->kyx", real_in, cosine, precision=highest)
        + jnp.einsum("yxz,zk->kyx", imag_in, sine_table, precision=highest)
    ) * norm_scale
    imag_out = (
        jnp.einsum("yxz,zk->kyx", imag_in, cosine, precision=highest)
        - jnp.einsum("yxz,zk->kyx", real_in, sine_table, precision=highest)
    ) * norm_scale
    planes = jnp.stack([real_out, imag_out], axis=2).astype(jnp.bfloat16)
    slab_planes = lax.all_to_all(planes, "slab", split_axis=0, concat_axis=1, tiled=True)
    gathered = lax.all_gather(slab_planes, "grp", axis=3, tiled=True)
    row_table = gathered.reshape(slab_depth * NF, 2 * NF)
    slot_map = send_map[0, 0]
    picked = jnp.take(row_table, jnp.maximum(slot_map, 0).reshape(-1), axis=0)
    picked = picked * (slot_map >= 0).reshape(-1, 1).astype(jnp.bfloat16)
    outgoing = picked.reshape(slot_map.shape[0], CAP, 2 * NF)
    arrived = lax.all_to_all(outgoing, "slab", split_axis=0, concat_axis=0, tiled=True)
    buffer = arrived.reshape(-1, 2 * NF)
    rows_local = interp_frac.shape[2]
    tap_index = interp_index[:, 0]
    weights_tap = interp_frac[0][..., None]
    lower_rows = jnp.take(buffer, tap_index[0].reshape(-1), axis=0).reshape(
        ORI_MAX, rows_local, 2 * NF
    )
    upper_rows = jnp.take(buffer, tap_index[1].reshape(-1), axis=0).reshape(
        ORI_MAX, rows_local, 2 * NF
    )
    slices = (1.0 - weights_tap) * lower_rows.astype(jnp.float32) + weights_tap * upper_rows.astype(
        jnp.float32
    )
    onehot = (class_ids[:, None] == jnp.arange(CLASSES, dtype=jnp.int32)[None, :]).astype(
        jnp.bfloat16
    )
    ctf_rows = jnp.dot(
        onehot, ctf_table.reshape(CLASSES, -1), preferred_element_type=jnp.float32
    ).reshape(PART_DEV, rows_local, NF)
    weighted = (
        (jnp.concatenate([ctf_rows, ctf_rows], axis=-1) * spectra.astype(jnp.float32))
        .astype(jnp.bfloat16)
        .reshape(PART_DEV, -1)
    )
    first_row = lax.axis_index("grp") * rows_local
    factors = phase_factors(first_row, rows_local)
    live_count = ori_count[0]

    def orient_score(orient):
        result = shift_score(slices[orient], weighted, factors)
        return jnp.where(orient < live_count, result, jnp.zeros_like(result))

    blocks_out = lax.map(orient_score, jnp.arange(ORI_MAX, dtype=jnp.int32))
    partial_scores = jnp.transpose(blocks_out, (1, 0, 2)).reshape(PART_DEV, ORI_MAX * TRANS)
    return lax.psum_scatter(partial_scores, "grp", scatter_dimension=1, tiled=True)


MESH = pl.DeviceIdType.MESH
CAP_FAST = 32


def dft_table():
    turns = np.outer(np.arange(NF), np.arange(NF)) % NF
    angle = 2.0 * np.pi / NF * turns
    cos, sin = np.cos(angle) / math.sqrt(NF), np.sin(angle) / math.sqrt(NF)
    return np.block([[cos, sin], [-sin, cos]]).astype(jnp.bfloat16)


def column_phases():
    side = np.arange(TSIDE) - TSIDE // 2
    angle = 2.0 * np.pi / NF * (np.outer(np.arange(NF), side) % NF)
    cos, sin = np.tile(np.cos(angle), (1, TSIDE)), np.tile(np.sin(angle), (1, TSIDE))
    full = np.block([[cos, -sin], [sin, cos]]).astype(np.float32)
    high = full.astype(jnp.bfloat16)
    low = (full - high.astype(np.float32)).astype(jnp.bfloat16)
    both = np.concatenate([high, low], axis=1).reshape(2, 2, 128, 256)
    return both.transpose(1, 0, 2, 3).reshape(2, NF, 256)


def row_phases():
    side = np.arange(TSIDE) - TSIDE // 2
    angle = 2.0 * np.pi / NF * (np.outer(np.arange(NF), side) % NF)
    cos, sin = np.repeat(np.cos(angle), TSIDE, 1), np.repeat(np.sin(angle), TSIDE, 1)
    return np.concatenate([cos, sin], axis=1).astype(np.float32)


def iota(shape, axis):
    return lax.broadcasted_iota(jnp.int32, shape, axis)


def fused(
    n_slab, n_grp, cap,
    class_hbm, count_hbm, map_hbm, index_hbm, frac_hbm, pencils, dft, spectra, ctf, phase_v, phase_u,
    out, load_out,
    maps, lines, table_w, planes, spec_in, ctf_in, col_ph, row_ph, rank_ref, key_ref, picked2, sendbuf,
    recv, weighted, product, part_send, part_recv, class_ids, ori_count, send_map, index, frac,
    load_sem, line_sem, map_send, map_recv, row_send, row_recv, sum_send, sum_recv,
):
    s, g = lax.axis_index("slab"), lax.axis_index("grp")
    ky_loc, kx_loc = pencils.shape[0], pencils.shape[1]
    rows_u = spectra.shape[1]
    slots = n_slab * CAP
    chunks = lines.shape[0]
    step = ky_loc // chunks
    peers = [(dg, ds) for dg in range(n_grp) for ds in range(n_slab) if dg + ds > 0]

    x, core = g // 2, g % 2
    order = [(1 - x) * 2 + core, (1 - x) * 2 + 1 - core, x * 2 + 1 - core, g]

    def peer(dg, ds):
        return lax.rem(s + ds, n_slab), lax.rem(g + dg, n_grp)

    barrier = pltpu.get_barrier_semaphore()
    for dg, ds in peers:
        pl.semaphore_signal(barrier, inc=1, device_id=peer(dg, ds), device_id_type=MESH)
    loads = [
        pltpu.make_async_copy(a, b, load_sem.at[i])
        for i, (a, b) in enumerate(
            [(map_hbm, send_map), (dft, table_w), (class_hbm, class_ids), (count_hbm, ori_count),
             (index_hbm, index), (frac_hbm, frac), (ctf, ctf_in), (spectra, spec_in), (phase_v, col_ph),
             (phase_u.at[pl.ds(pl.multiple_of(g * rows_u, rows_u), rows_u)], row_ph)]
        )
    ]

    def line_load(c):
        return pltpu.make_async_copy(pencils.at[pl.ds(c * step, step)], lines.at[c], line_sem.at[c])

    for copy in loads[:2]:
        copy.start()
    for c in range(chunks):
        line_load(c).start()
    for copy in loads[2:]:
        copy.start()

    def transform(c, carry):
        line_load(c).wait()
        block = lines[c].reshape(step * kx_loc, 2 * NF).astype(jnp.bfloat16)
        lanes = lax.dot_general(
            table_w[...], block, (((1,), (1,)), ((), ())), preferred_element_type=jnp.float32
        ).astype(jnp.bfloat16)
        for h in range(step // 2):
            planes[c * (step // 2) + h, :, :128] = lanes[:NF, h * 128:(h + 1) * 128]
            planes[c * (step // 2) + h, :, 128:] = lanes[NF:, h * 128:(h + 1) * 128]
        return carry

    loads[1].wait()
    for c in range(chunks // 2):
        transform(c, 0)
    loads[0].wait()
    maps[s, g] = jnp.concatenate([send_map[...]] * n_slab, axis=1)
    pl.semaphore_wait(barrier, len(peers))

    def map_copy(to, whose):
        return pltpu.make_async_remote_copy(
            src_ref=maps.at[s, g], dst_ref=maps.at[whose[0], whose[1]],
            send_sem=map_send.at[to[0], to[1]], recv_sem=map_recv.at[whose[0], whose[1]],
            device_id=to, device_id_type=MESH)

    for dg, ds in peers:
        map_copy(peer(dg, ds), (s, g)).start()

    for c in range(chunks // 2, chunks):
        transform(c, 0)

    for dg, ds in peers:
        whose = peer(dg, ds)
        map_copy(whose, whose).wait_recv()

    lane = iota((n_slab, slots), 1)
    rows = jnp.concatenate(
        [sum(jnp.where(lane // CAP == a, maps[a, b], 0) for a in range(n_slab)) for b in range(n_grp)],
        axis=0,
    )
    shift = ky_loc.bit_length() - 1
    used = rows >= 0
    ky = rows & (NF - 1)
    home = jnp.where(used, ky >> shift, -1)
    tri = (iota((slots, slots), 0) < iota((slots, slots), 1)).astype(jnp.float32).astype(jnp.bfloat16)

    def ranks(mask):
        ones = jnp.where(mask, 1.0, 0.0)
        return jnp.dot(ones.astype(jnp.bfloat16), tri, preferred_element_type=jnp.float32), ones

    mine = home == s
    rank, _ = ranks(mine)
    rank = jnp.where(mine, rank, -1.0)
    ky_own = ky & (ky_loc - 1)
    kz = (iota(rows.shape, 1) // CAP) * (NF // n_slab) + (rows >> 8)
    code = (((ky_own >> 1) * NF + kz) * 2 + (ky_own & 1) + 1).astype(jnp.float32)
    for b in range(n_grp):
        rank_ref[b] = rank[b * n_slab:(b + 1) * n_slab]
        key_ref[b] = code[b * n_slab:(b + 1) * n_slab]
    most = jnp.zeros((rows.shape[0], 1), jnp.float32)
    for a in range(n_slab):
        most = jnp.maximum(most, jnp.sum(jnp.where(home == a, 1.0, 0.0), axis=1, keepdims=True))
    load_out[0] = (jnp.max(most) > cap).astype(jnp.int32)

    def row_copy(to, whose):
        return pltpu.make_async_remote_copy(
            src_ref=sendbuf.at[to[1], to[0]],
            dst_ref=recv.at[whose[1], pl.ds(pl.multiple_of(whose[0] * cap, cap), cap)],
            send_sem=row_send.at[to[1], to[0]], recv_sem=row_recv.at[whose[1], whose[0]],
            device_id=to, device_id_type=MESH)

    pairs = ky_loc // 2
    at_once = 256 // cap
    lane256 = iota((256, NF), 1)
    lane128 = iota((256, 128), 1)

    def pick(i):
        to_g = order[i]
        picked = picked2.at[i % 2]
        for q in range(n_slab // at_once):
            rk = rank_ref[to_g, q * at_once:(q + 1) * at_once]
            cd = key_ref[to_g, q * at_once:(q + 1) * at_once]
            places = iota((at_once, cap, slots), 1).astype(jnp.float32)
            hit = jnp.where(rk[:, None, :] == places, cd[:, None, :], 0.0)
            found = (jnp.sum(hit, axis=2, keepdims=True) - 1.0).reshape(256, 1).astype(jnp.int32)
            odd = (found & 1) == 1
            pair = jnp.broadcast_to((found >> (NF.bit_length())).astype(jnp.float32), (256, NF)).astype(jnp.bfloat16)
            plane_hit = jnp.where(((found >> 1) & (NF - 1)) == lane256, 1.0, 0.0).astype(jnp.bfloat16)
            for j in range(pairs):
                picked[:, j * NF:(j + 1) * NF] = jnp.where(
                    pair == jnp.bfloat16(j), plane_hit, jnp.bfloat16(0))
            got = jnp.dot(picked[...], planes[...].reshape(pairs * NF, 256),
                          preferred_element_type=jnp.float32)
            a, b = got[:, :128], got[:, 128:]
            row = jnp.where(lane128 < 64, jnp.where(odd, pltpu.roll(a, 64, 1), a),
                            jnp.where(odd, b, pltpu.roll(b, 64, 1)))
            sendbuf[to_g, q * at_once:(q + 1) * at_once] = row.astype(jnp.bfloat16).reshape(at_once, cap, 128)
        for ds in sorted(range(n_slab), key=lambda d: -min(d, n_slab - d)):
            if i < n_grp - 1 or ds > 0:
                row_copy((lax.rem(s + ds, n_slab), to_g), (s, g)).start()

    for i in range(n_grp):
        pick(i)
    recv[g, pl.ds(pl.multiple_of(s * cap, cap), cap)] = sendbuf[g, s]

    for copy in loads[2:]:
        copy.wait()
    for p in range(PART_DEV):
        for h in range(2):
            ctf_rows = ctf_in[class_ids[p], :, h * 128:(h + 1) * 128].astype(jnp.float32)
            for part in range(2):
                at = part * NF + h * 128
                weighted[h, p, :, part * 128:(part + 1) * 128] = (
                    ctf_rows * spec_in[p, :, at:at + 128].astype(jnp.float32)
                ).astype(jnp.bfloat16)

    own = jnp.sum(jnp.where(lane // CAP == iota((n_slab, slots), 0), maps_row(maps, s, g, n_slab), 0),
                  axis=0, keepdims=True)
    own_home = jnp.where(own >= 0, (own & (NF - 1)) >> shift, -1)
    from_a = own_home == iota((n_slab, slots), 0)
    own_rank, ones = ranks(from_a)
    base = (iota((n_slab, slots), 0) * cap).astype(jnp.float32)
    place = jnp.sum(ones * (own_rank + base + 1.0), axis=0, keepdims=True) - 1.0
    spread = jnp.where(place == iota((n_slab * cap, slots), 0).astype(jnp.float32), 1.0, 0.0).astype(jnp.bfloat16)

    for dg, ds in peers:
        map_copy(peer(dg, ds), (s, g)).wait_send()
    lane_s = iota((slots, 128), 1)

    def lists(half, turn):
        got = []
        for b in range(2):
            from_g = half * 2 + b
            got.append(lax.dot_general(spread, recv[from_g], (((0,), (0,)), ((), ())),
                                       preferred_element_type=jnp.float32))
        a, b = got
        block = jnp.concatenate([jnp.where(lane_s < 64, a, pltpu.roll(b, 64, 1)),
                                 jnp.where(lane_s < 64, pltpu.roll(a, 64, 1), b)], axis=1)
        block = block.astype(jnp.bfloat16)
        return jnp.concatenate([block, block], axis=0)

    def sum_copy(to_g, whose_g):
        return pltpu.make_async_remote_copy(
            src_ref=part_send.at[to_g], dst_ref=part_recv.at[whose_g],
            send_sem=sum_send.at[to_g], recv_sem=sum_recv.at[whose_g],
            device_id=(s, to_g), device_id_type=MESH)

    slot_id = iota((slots, rows_u), 0)
    live = ori_count[0]
    lane_p = iota((PART_DEV, 128), 1)

    def half_score(o, half, received, buf):
        i0 = index[0, pl.ds(o, 1), :]
        i1 = index[1, pl.ds(o, 1), :]
        w = frac[pl.ds(o, 1), :]
        taps = jnp.where(slot_id == i0, 1.0 - w, 0.0) + jnp.where(slot_id == i1, w, 0.0)
        high = taps.astype(jnp.bfloat16)
        low = (taps - high.astype(jnp.float32)).astype(jnp.bfloat16)
        rows_o = lax.dot_general(
            jnp.concatenate([high, low], axis=0), received, (((0,), (0,)), ((), ())),
            preferred_element_type=jnp.float32)
        sr, si = rows_o[:, :128], rows_o[:, 128:]
        for p in range(PART_DEV):
            wr = weighted[half, p, :, :128].astype(jnp.float32)
            wi = weighted[half, p, :, 128:].astype(jnp.float32)
            product[buf, p * rows_u:(p + 1) * rows_u, :128] = (wr * sr + wi * si).astype(jnp.bfloat16)
            product[buf, p * rows_u:(p + 1) * rows_u, 128:] = (wr * si - wi * sr).astype(jnp.bfloat16)
        z = jnp.dot(product[buf], col_ph[half], preferred_element_type=jnp.float32)
        z = (z[:, :128] + z[:, 128:]).reshape(PART_DEV, rows_u, 128)
        return jnp.sum(z * row_ph[...][None], axis=1)

    partial = {}
    for turn, half in enumerate([1 - x, x]):
        for i in (0, 1) if turn == 0 else (2, 3):
            for ds in range(n_slab):
                if i < n_grp - 1 or ds > 0:
                    whose = (lax.rem(s + ds, n_slab), order[i])
                    row_copy(whose, whose).wait_recv()
        received = lists(half, turn)
        for i in range(n_grp):
            to_g = order[i]
            folded = []
            for e in range(2):
                o = to_g * 2 + e
                t = half_score(o, half, received, e)
                if turn == 0:
                    partial[i, e] = t
                else:
                    t = partial[i, e] + t
                    t = (t + pltpu.roll(t, 64, 1)) * (1.0 / NF)
                    folded.append(jnp.where(o < live, t, 0.0))
            if turn == 1:
                part_send[to_g] = jnp.where(lane_p < 64, folded[0], folded[1])
                if i < n_grp - 1:
                    sum_copy(to_g, g).start()
    for dg, ds in peers:
        row_copy(peer(dg, ds), (s, g)).wait_send()
    total = part_send[g]
    for dg in range(1, n_grp):
        from_g = lax.rem(g + dg, n_grp)
        sum_copy(from_g, from_g).wait_recv()
        total += part_recv[from_g]
    out[...] = total
    for dg in range(1, n_grp):
        sum_copy(lax.rem(g + dg, n_grp), g).wait_send()


def maps_row(maps, s, g, n_slab):
    return jnp.concatenate([maps[a, g, pl.ds(s, 1), :] for a in range(n_slab)], axis=0)


def run_fused(n_slab, n_grp, cap, collective_id, args):
    pencils, send_map, index, frac, ori_count, spectra, class_ids, ctf = args
    ky_loc, kx_loc = pencils.shape[:2]
    rows_u = spectra.shape[1]
    slots = n_slab * CAP
    chunks = ky_loc // 4
    vmem, smem, hbm = (pl.BlockSpec(memory_space=m) for m in (pltpu.VMEM, pltpu.SMEM, pl.ANY))
    dma = pltpu.SemaphoreType.DMA
    return pl.pallas_call(
        lambda *refs: fused(n_slab, n_grp, cap, *refs),
        out_shape=[
            jax.ShapeDtypeStruct((PART_DEV, ORI_MAX * TRANS // n_grp), jnp.float32),
            jax.ShapeDtypeStruct((1,), jnp.int32),
        ],
        in_specs=[hbm] * 11,
        out_specs=[vmem, smem],
        scratch_shapes=[
            pltpu.VMEM((n_slab, n_grp, n_slab, slots), jnp.int32),
            pltpu.VMEM((chunks, 4, kx_loc, 2 * NF), jnp.float32),
            pltpu.VMEM((2 * NF, 2 * NF), jnp.bfloat16),
            pltpu.VMEM((ky_loc // 2, NF, 256), jnp.bfloat16),
            pltpu.VMEM(spectra.shape, jnp.bfloat16),
            pltpu.VMEM(ctf.shape, jnp.bfloat16),
            pltpu.VMEM((2, NF, 256), jnp.bfloat16),
            pltpu.VMEM((rows_u, 128), jnp.float32),
            pltpu.VMEM((n_grp, n_slab, slots), jnp.float32),
            pltpu.VMEM((n_grp, n_slab, slots), jnp.float32),
            pltpu.VMEM((2, 256, ky_loc // 2 * NF), jnp.bfloat16),
            pltpu.VMEM((n_grp, n_slab, cap, 128), jnp.bfloat16),
            pltpu.VMEM((n_grp, n_slab * cap, 128), jnp.bfloat16),
            pltpu.VMEM((2, PART_DEV, rows_u, NF), jnp.bfloat16),
            pltpu.VMEM((2, PART_DEV * rows_u, NF), jnp.bfloat16),
            pltpu.VMEM((n_grp, PART_DEV, 128), jnp.float32),
            pltpu.VMEM((n_grp, PART_DEV, 128), jnp.float32),
            pltpu.SMEM(class_ids.shape, jnp.int32),
            pltpu.SMEM(ori_count.shape, jnp.int32),
            pltpu.VMEM(send_map.shape[2:], jnp.int32),
            pltpu.VMEM((2, ORI_MAX, rows_u), jnp.int32),
            pltpu.VMEM((ORI_MAX, rows_u), jnp.float32),
            dma((10,)),
            dma((chunks,)),
            dma((n_slab, n_grp)),
            dma((n_slab, n_grp)),
            dma((n_grp, n_slab)),
            dma((n_grp, n_slab)),
            dma((n_grp,)),
            dma((n_grp,)),
        ],
        compiler_params=pltpu.CompilerParams(
            collective_id=collective_id, has_side_effects=True, vmem_limit_bytes=60 * 2**20),
    )(
        class_ids, ori_count, send_map[0, 0], index[:, 0], frac[0], pencils, jnp.asarray(dft_table()),
        spectra, ctf, jnp.asarray(column_phases()), jnp.asarray(row_phases()),
    )


def listed(n_slab, n_grp, *args):
    scores, load = run_fused(n_slab, n_grp, CAP_FAST, 1, args)
    return lax.cond(
        load.reshape(()) > 0,
        lambda: run_fused(n_slab, n_grp, n_slab * CAP, 2, args)[0],
        lambda: scores,
    )


def solution(mesh):
    n_slab, n_grp = mesh.shape["slab"], mesh.shape["grp"]

    def body(*args):
        if n_slab * CAP == 128 and n_grp == 4:
            return listed(n_slab, n_grp, *args)
        return shards(*args)

    return jax.shard_map(
        body,
        mesh=mesh,
        in_specs=(
            P("slab", "grp", None),
            P("slab", "grp", None, None),
            P(None, "slab", None, "grp"),
            P("slab", None, "grp"),
            P("slab"),
            P("slab", "grp", None),
            P("slab"),
            P(None, "grp", None),
        ),
        out_specs=P("slab", "grp"),
        check_vma=False,
    )
```

```python
import math

import jax
import jax.numpy as jnp
import numpy as np
from jax import lax
from jax.experimental import pallas as pl
from jax.experimental.pallas import tpu as pltpu
from jax.sharding import PartitionSpec as P

NF = 256
CAP = 16
ORI_MAX = 8
TSIDE = 8
CLASSES = 16
PART_DEV = 8
TRANS = 64


def phase_factors(first_row, row_total):
    side_ids = jnp.arange(TSIDE, dtype=jnp.int32) - TSIDE // 2
    rows_u = first_row + jnp.arange(row_total, dtype=jnp.int32)
    cols_v = jnp.arange(NF, dtype=jnp.int32)
    turns_u = side_ids[:, None] * rows_u[None, :] % NF
    turns_v = side_ids[:, None] * cols_v[None, :] % NF
    angle_u = -2.0 * math.pi / NF * turns_u.astype(jnp.float32)
    angle_v = -2.0 * math.pi / NF * turns_v.astype(jnp.float32)
    return (jnp.cos(angle_u), jnp.sin(angle_u), jnp.cos(angle_v), jnp.sin(angle_v))


def shift_score(slice_rows, weighted, factors):
    cos_u, sin_u, cos_v, sin_v = factors
    row_total = slice_rows.shape[0]
    cu = cos_u[:, None, :, None]
    su = sin_u[:, None, :, None]
    cv = cos_v[None, :, None, :]
    sv = sin_v[None, :, None, :]
    cosines = (cu * cv - su * sv).reshape(TRANS, row_total, NF)
    sines = (su * cv + cu * sv).reshape(TRANS, row_total, NF)
    real_part = slice_rows[None, :, :NF]
    imag_part = slice_rows[None, :, NF:]
    shifted = jnp.concatenate(
        [real_part * cosines - imag_part * sines, real_part * sines + imag_part * cosines], axis=-1
    ).astype(jnp.bfloat16)
    flat_refs = shifted.reshape(TRANS, -1)
    return (
        lax.dot_general(
            weighted, flat_refs, (((1,), (1,)), ((), ())), preferred_element_type=jnp.float32
        )
        / NF
    )


def shards(pencils, send_map, interp_index, interp_frac, ori_count, spectra, class_ids, ctf_table):
    slab_depth = NF // lax.axis_size("slab")
    freq_index = jnp.arange(NF, dtype=jnp.int32)
    phase_turns = freq_index[:, None] * freq_index[None, :] % NF
    angles = 2.0 * math.pi / NF * phase_turns.astype(jnp.float32)
    cosine = jnp.cos(angles)
    sine_table = jnp.sin(angles)
    norm_scale = 1.0 / math.sqrt(NF)
    real_in = pencils[..., :NF]
    imag_in = pencils[..., NF:]
    highest = lax.Precision.HIGHEST
    real_out = (
        jnp.einsum("yxz,zk->kyx", real_in, cosine, precision=highest)
        + jnp.einsum("yxz,zk->kyx", imag_in, sine_table, precision=highest)
    ) * norm_scale
    imag_out = (
        jnp.einsum("yxz,zk->kyx", imag_in, cosine, precision=highest)
        - jnp.einsum("yxz,zk->kyx", real_in, sine_table, precision=highest)
    ) * norm_scale
    planes = jnp.stack([real_out, imag_out], axis=2).astype(jnp.bfloat16)
    slab_planes = lax.all_to_all(planes, "slab", split_axis=0, concat_axis=1, tiled=True)
    gathered = lax.all_gather(slab_planes, "grp", axis=3, tiled=True)
    row_table = gathered.reshape(slab_depth * NF, 2 * NF)
    slot_map = send_map[0, 0]
    picked = jnp.take(row_table, jnp.maximum(slot_map, 0).reshape(-1), axis=0)
    picked = picked * (slot_map >= 0).reshape(-1, 1).astype(jnp.bfloat16)
    outgoing = picked.reshape(slot_map.shape[0], CAP, 2 * NF)
    arrived = lax.all_to_all(outgoing, "slab", split_axis=0, concat_axis=0, tiled=True)
    buffer = arrived.reshape(-1, 2 * NF)
    rows_local = interp_frac.shape[2]
    tap_index = interp_index[:, 0]
    weights_tap = interp_frac[0][..., None]
    lower_rows = jnp.take(buffer, tap_index[0].reshape(-1), axis=0).reshape(
        ORI_MAX, rows_local, 2 * NF
    )
    upper_rows = jnp.take(buffer, tap_index[1].reshape(-1), axis=0).reshape(
        ORI_MAX, rows_local, 2 * NF
    )
    slices = (1.0 - weights_tap) * lower_rows.astype(jnp.float32) + weights_tap * upper_rows.astype(
        jnp.float32
    )
    onehot = (class_ids[:, None] == jnp.arange(CLASSES, dtype=jnp.int32)[None, :]).astype(
        jnp.bfloat16
    )
    ctf_rows = jnp.dot(
        onehot, ctf_table.reshape(CLASSES, -1), preferred_element_type=jnp.float32
    ).reshape(PART_DEV, rows_local, NF)
    weighted = (
        (jnp.concatenate([ctf_rows, ctf_rows], axis=-1) * spectra.astype(jnp.float32))
        .astype(jnp.bfloat16)
        .reshape(PART_DEV, -1)
    )
    first_row = lax.axis_index("grp") * rows_local
    factors = phase_factors(first_row, rows_local)
    live_count = ori_count[0]

    def orient_score(orient):
        result = shift_score(slices[orient], weighted, factors)
        return jnp.where(orient < live_count, result, jnp.zeros_like(result))

    blocks_out = lax.map(orient_score, jnp.arange(ORI_MAX, dtype=jnp.int32))
    partial_scores = jnp.transpose(blocks_out, (1, 0, 2)).reshape(PART_DEV, ORI_MAX * TRANS)
    return lax.psum_scatter(partial_scores, "grp", scatter_dimension=1, tiled=True)


MESH = pl.DeviceIdType.MESH
CAP_FAST = 32


def dft_table():
    turns = np.outer(np.arange(NF), np.arange(NF)) % NF
    angle = 2.0 * np.pi / NF * turns
    cos, sin = np.cos(angle) / math.sqrt(NF), np.sin(angle) / math.sqrt(NF)
    return np.block([[cos, sin], [-sin, cos]]).astype(jnp.bfloat16)


def column_phases():
    side = np.arange(TSIDE) - TSIDE // 2
    angle = 2.0 * np.pi / NF * (np.outer(np.arange(NF), side) % NF)
    cos, sin = np.tile(np.cos(angle), (1, TSIDE)), np.tile(np.sin(angle), (1, TSIDE))
    full = np.block([[cos, -sin], [sin, cos]]).astype(np.float32)
    high = full.astype(jnp.bfloat16)
    low = (full - high.astype(np.float32)).astype(jnp.bfloat16)
    both = np.concatenate([high, low], axis=1).reshape(2, 2, 128, 256)
    return both.transpose(1, 0, 2, 3).reshape(2, NF, 256)


def row_phases():
    side = np.arange(TSIDE) - TSIDE // 2
    angle = 2.0 * np.pi / NF * (np.outer(np.arange(NF), side) % NF)
    cos, sin = np.repeat(np.cos(angle), TSIDE, 1), np.repeat(np.sin(angle), TSIDE, 1)
    return np.concatenate([cos, sin], axis=1).astype(np.float32)


def iota(shape, axis):
    return lax.broadcasted_iota(jnp.int32, shape, axis)


def fused(
    n_slab, n_grp, cap,
    class_hbm, count_hbm, map_hbm, index_hbm, frac_hbm, pencils, dft, spectra, ctf, phase_v, phase_u,
    out, load_out,
    maps, lines, table_w, planes, spec_in, ctf_in, col_ph, row_ph, rank_ref, key_ref, picked2, sendbuf,
    recv, weighted, product, part_send, part_recv, class_ids, ori_count, send_map, index, frac,
    load_sem, line_sem, hop_send, hop_recv, map_send, map_recv, row_send, row_recv, sum_send, sum_recv,
):
    s, g = lax.axis_index("slab"), lax.axis_index("grp")
    ky_loc, kx_loc = pencils.shape[0], pencils.shape[1]
    rows_u = spectra.shape[1]
    slots = n_slab * CAP
    chunks = lines.shape[0]
    step = ky_loc // chunks
    peers = [(dg, ds) for dg in range(n_grp) for ds in range(n_slab) if dg + ds > 0]

    x, core = g // 2, g % 2
    order = [(1 - x) * 2 + core, (1 - x) * 2 + 1 - core, x * 2 + 1 - core, g]

    def peer(dg, ds):
        return lax.rem(s + ds, n_slab), lax.rem(g + dg, n_grp)

    barrier = pltpu.get_barrier_semaphore()
    deep = n_slab // 2
    z, y = s // 2, s % 2
    beside = [(z * 2 + 1 - y, g)] + [peer(dg, 0) for dg in range(1, n_grp)]
    for to in beside:
        pl.semaphore_signal(barrier, inc=1, device_id=to, device_id_type=MESH)

    @pl.when(z > 0)
    def _():
        pl.semaphore_signal(barrier, inc=1, device_id=(s - 2, g), device_id_type=MESH)

    @pl.when(z < deep - 1)
    def _():
        pl.semaphore_signal(barrier, inc=1, device_id=(s + 2, g), device_id_type=MESH)

    loads = [
        pltpu.make_async_copy(a, b, load_sem.at[i])
        for i, (a, b) in enumerate(
            [(map_hbm, send_map), (dft, table_w), (class_hbm, class_ids), (count_hbm, ori_count),
             (index_hbm, index), (frac_hbm, frac), (ctf, ctf_in), (spectra, spec_in), (phase_v, col_ph),
             (phase_u.at[pl.ds(pl.multiple_of(g * rows_u, rows_u), rows_u)], row_ph)]
        )
    ]

    def line_load(c):
        return pltpu.make_async_copy(pencils.at[pl.ds(c * step, step)], lines.at[c], line_sem.at[c])

    for copy in loads[:2]:
        copy.start()
    for c in range(chunks):
        line_load(c).start()
    for copy in loads[2:]:
        copy.start()

    def transform(c, carry):
        line_load(c).wait()
        block = lines[c].reshape(step * kx_loc, 2 * NF).astype(jnp.bfloat16)
        lanes = lax.dot_general(
            table_w[...], block, (((1,), (1,)), ((), ())), preferred_element_type=jnp.float32
        ).astype(jnp.bfloat16)
        for h in range(step // 2):
            planes[c * (step // 2) + h, :, :128] = lanes[:NF, h * 128:(h + 1) * 128]
            planes[c * (step // 2) + h, :, 128:] = lanes[NF:, h * 128:(h + 1) * 128]
        return carry

    loads[0].wait()
    tiled = jnp.concatenate([send_map[...]] * n_slab, axis=1)
    lane = iota((n_slab, slots), 1)
    maps[g, y, z] = jnp.sum(jnp.where(lane // CAP == iota((n_slab, slots), 0), tiled, 0), axis=0, keepdims=True)
    pl.semaphore_wait(barrier, len(beside) + jnp.minimum(z, 1) + jnp.minimum(deep - 1 - z, 1))

    def hop(block, step):
        return pltpu.make_async_remote_copy(
            src_ref=maps.at[g, y, block], dst_ref=maps.at[g, y, block],
            send_sem=hop_send.at[(step + 1) // 2, block], recv_sem=hop_recv.at[block],
            device_id=(s + 2 * step, g), device_id_type=MESH)

    def for_hops(turn, act):
        @pl.when((z - turn >= 0) & (z < deep - 1))
        def _():
            act(hop(z - turn, 1))

        @pl.when((z + turn <= deep - 1) & (z > 0))
        def _():
            act(hop(z + turn, -1))

    def hops_arrive(turn):
        def arrive(block):
            pltpu.make_async_remote_copy(
                src_ref=maps.at[g, y, block], dst_ref=maps.at[g, y, block], send_sem=hop_send.at[0, block],
                recv_sem=hop_recv.at[block], device_id=beside[0], device_id_type=MESH).wait_recv()

        @pl.when(z - turn >= 0)
        def _():
            arrive(z - turn)

        @pl.when(z + turn <= deep - 1)
        def _():
            arrive(z + turn)

    for turn in range(deep):
        if turn > 0:
            hops_arrive(turn)
        if turn < deep - 1:
            for_hops(turn, lambda copy: copy.start())
        else:
            over_y = pltpu.make_async_remote_copy(
                src_ref=maps.at[g, y], dst_ref=maps.at[g, y], send_sem=map_send.at[0],
                recv_sem=map_recv.at[0], device_id=beside[0], device_id_type=MESH)
            over_y.start()
        if turn == 0:
            loads[1].wait()
        for c in range(chunks * turn // deep, chunks * (turn + 1) // deep):
            transform(c, 0)
    over_y_in = pltpu.make_async_remote_copy(
        src_ref=maps.at[g, 1 - y], dst_ref=maps.at[g, 1 - y], send_sem=map_send.at[0],
        recv_sem=map_recv.at[0], device_id=beside[0], device_id_type=MESH)
    over_y_in.wait_recv()

    def over_grp(to_g, whose_g):
        return pltpu.make_async_remote_copy(
            src_ref=maps.at[whose_g], dst_ref=maps.at[whose_g], send_sem=map_send.at[1 + to_g],
            recv_sem=map_recv.at[1 + whose_g], device_id=(s, to_g), device_id_type=MESH)

    for dg in range(1, n_grp):
        over_grp(lax.rem(g + dg, n_grp), g).start()
    for dg in range(1, n_grp):
        from_g = lax.rem(g + dg, n_grp)
        over_grp(from_g, from_g).wait_recv()

    def unfold(b):
        stack = jnp.concatenate(
            [jnp.where(lane // CAP == iota((n_slab, slots), 0), maps[b, a % 2, a // 2], 0) for a in range(n_slab)],
            axis=0)
        for k in (64, 32, 16):
            stack = stack + pltpu.roll(stack, k, 1)
        return sum(jnp.where(lane // CAP == a, stack[a * n_slab:(a + 1) * n_slab], 0) for a in range(n_slab))

    rows = jnp.concatenate([unfold(b) for b in range(n_grp)], axis=0)
    shift = ky_loc.bit_length() - 1
    used = rows >= 0
    ky = rows & (NF - 1)
    home = jnp.where(used, ky >> shift, -1)
    tri = (iota((slots, slots), 0) < iota((slots, slots), 1)).astype(jnp.float32).astype(jnp.bfloat16)

    def ranks(mask):
        ones = jnp.where(mask, 1.0, 0.0)
        return jnp.dot(ones.astype(jnp.bfloat16), tri, preferred_element_type=jnp.float32), ones

    mine = home == s
    rank, _ = ranks(mine)
    rank = jnp.where(mine, rank, -1.0)
    ky_own = ky & (ky_loc - 1)
    kz = (iota(rows.shape, 1) // CAP) * (NF // n_slab) + (rows >> 8)
    code = (((ky_own >> 1) * NF + kz) * 2 + (ky_own & 1) + 1).astype(jnp.float32)
    for b in range(n_grp):
        rank_ref[b] = rank[b * n_slab:(b + 1) * n_slab]
        key_ref[b] = code[b * n_slab:(b + 1) * n_slab]
    most = jnp.zeros((rows.shape[0], 1), jnp.float32)
    for a in range(n_slab):
        most = jnp.maximum(most, jnp.sum(jnp.where(home == a, 1.0, 0.0), axis=1, keepdims=True))
    load_out[0] = (jnp.max(most) > cap).astype(jnp.int32)

    def row_copy(to, whose):
        return pltpu.make_async_remote_copy(
            src_ref=sendbuf.at[to[1], to[0]],
            dst_ref=recv.at[whose[1], pl.ds(pl.multiple_of(whose[0] * cap, cap), cap)],
            send_sem=row_send.at[to[1], to[0]], recv_sem=row_recv.at[whose[1], whose[0]],
            device_id=to, device_id_type=MESH)

    pairs = ky_loc // 2
    at_once = 256 // cap
    lane256 = iota((256, NF), 1)
    lane128 = iota((256, 128), 1)

    def pick(i):
        to_g = order[i]
        picked = picked2.at[i % 2]
        for q in range(n_slab // at_once):
            rk = rank_ref[to_g, q * at_once:(q + 1) * at_once]
            cd = key_ref[to_g, q * at_once:(q + 1) * at_once]
            places = iota((at_once, cap, slots), 1).astype(jnp.float32)
            hit = jnp.where(rk[:, None, :] == places, cd[:, None, :], 0.0)
            found = (jnp.sum(hit, axis=2, keepdims=True) - 1.0).reshape(256, 1).astype(jnp.int32)
            odd = (found & 1) == 1
            pair = jnp.broadcast_to((found >> (NF.bit_length())).astype(jnp.float32), (256, NF)).astype(jnp.bfloat16)
            plane_hit = jnp.where(((found >> 1) & (NF - 1)) == lane256, 1.0, 0.0).astype(jnp.bfloat16)
            for j in range(pairs):
                picked[:, j * NF:(j + 1) * NF] = jnp.where(
                    pair == jnp.bfloat16(j), plane_hit, jnp.bfloat16(0))
            got = jnp.dot(picked[...], planes[...].reshape(pairs * NF, 256),
                          preferred_element_type=jnp.float32)
            a, b = got[:, :128], got[:, 128:]
            row = jnp.where(lane128 < 64, jnp.where(odd, pltpu.roll(a, 64, 1), a),
                            jnp.where(odd, b, pltpu.roll(b, 64, 1)))
            sendbuf[to_g, q * at_once:(q + 1) * at_once] = row.astype(jnp.bfloat16).reshape(at_once, cap, 128)
        for ds in sorted(range(n_slab), key=lambda d: -min(d, n_slab - d)):
            if i < n_grp - 1 or ds > 0:
                row_copy((lax.rem(s + ds, n_slab), to_g), (s, g)).start()

    for i in range(n_grp):
        pick(i)
    recv[g, pl.ds(pl.multiple_of(s * cap, cap), cap)] = sendbuf[g, s]

    for copy in loads[2:]:
        copy.wait()
    for p in range(PART_DEV):
        for h in range(2):
            ctf_rows = ctf_in[class_ids[p], :, h * 128:(h + 1) * 128].astype(jnp.float32)
            for part in range(2):
                at = part * NF + h * 128
                weighted[h, p, :, part * 128:(part + 1) * 128] = (
                    ctf_rows * spec_in[p, :, at:at + 128].astype(jnp.float32)
                ).astype(jnp.bfloat16)

    own = jnp.sum(jnp.where(iota(rows.shape, 0) == g * n_slab + s, rows, 0), axis=0, keepdims=True)
    own_home = jnp.where(own >= 0, (own & (NF - 1)) >> shift, -1)
    from_a = own_home == iota((n_slab, slots), 0)
    own_rank, ones = ranks(from_a)
    base = (iota((n_slab, slots), 0) * cap).astype(jnp.float32)
    place = jnp.sum(ones * (own_rank + base + 1.0), axis=0, keepdims=True) - 1.0
    spread = jnp.where(place == iota((n_slab * cap, slots), 0).astype(jnp.float32), 1.0, 0.0).astype(jnp.bfloat16)

    for turn in range(deep - 1):
        for_hops(turn, lambda copy: copy.wait_send())
    over_y.wait_send()
    for dg in range(1, n_grp):
        over_grp(lax.rem(g + dg, n_grp), g).wait_send()
    lane_s = iota((slots, 128), 1)

    def lists(half, turn):
        got = []
        for b in range(2):
            from_g = half * 2 + b
            got.append(lax.dot_general(spread, recv[from_g], (((0,), (0,)), ((), ())),
                                       preferred_element_type=jnp.float32))
        a, b = got
        block = jnp.concatenate([jnp.where(lane_s < 64, a, pltpu.roll(b, 64, 1)),
                                 jnp.where(lane_s < 64, pltpu.roll(a, 64, 1), b)], axis=1)
        block = block.astype(jnp.bfloat16)
        return jnp.concatenate([block, block], axis=0)

    def sum_copy(to_g, whose_g):
        return pltpu.make_async_remote_copy(
            src_ref=part_send.at[to_g], dst_ref=part_recv.at[whose_g],
            send_sem=sum_send.at[to_g], recv_sem=sum_recv.at[whose_g],
            device_id=(s, to_g), device_id_type=MESH)

    slot_id = iota((slots, rows_u), 0)
    live = ori_count[0]
    lane_p = iota((PART_DEV, 128), 1)

    def half_score(o, half, received, buf):
        i0 = index[0, pl.ds(o, 1), :]
        i1 = index[1, pl.ds(o, 1), :]
        w = frac[pl.ds(o, 1), :]
        taps = jnp.where(slot_id == i0, 1.0 - w, 0.0) + jnp.where(slot_id == i1, w, 0.0)
        high = taps.astype(jnp.bfloat16)
        low = (taps - high.astype(jnp.float32)).astype(jnp.bfloat16)
        rows_o = lax.dot_general(
            jnp.concatenate([high, low], axis=0), received, (((0,), (0,)), ((), ())),
            preferred_element_type=jnp.float32)
        sr, si = rows_o[:, :128], rows_o[:, 128:]
        for p in range(PART_DEV):
            wr = weighted[half, p, :, :128].astype(jnp.float32)
            wi = weighted[half, p, :, 128:].astype(jnp.float32)
            product[buf, p * rows_u:(p + 1) * rows_u, :128] = (wr * sr + wi * si).astype(jnp.bfloat16)
            product[buf, p * rows_u:(p + 1) * rows_u, 128:] = (wr * si - wi * sr).astype(jnp.bfloat16)
        z = jnp.dot(product[buf], col_ph[half], preferred_element_type=jnp.float32)
        z = (z[:, :128] + z[:, 128:]).reshape(PART_DEV, rows_u, 128)
        return jnp.sum(z * row_ph[...][None], axis=1)

    partial = {}
    for turn, half in enumerate([1 - x, x]):
        for i in (0, 1) if turn == 0 else (2, 3):
            for ds in range(n_slab):
                if i < n_grp - 1 or ds > 0:
                    whose = (lax.rem(s + ds, n_slab), order[i])
                    row_copy(whose, whose).wait_recv()
        received = lists(half, turn)
        for i in range(n_grp):
            to_g = order[i]
            folded = []
            for e in range(2):
                o = to_g * 2 + e
                t = half_score(o, half, received, e)
                if turn == 0:
                    partial[i, e] = t
                else:
                    t = partial[i, e] + t
                    t = (t + pltpu.roll(t, 64, 1)) * (1.0 / NF)
                    folded.append(jnp.where(o < live, t, 0.0))
            if turn == 1:
                part_send[to_g] = jnp.where(lane_p < 64, folded[0], folded[1])
                if i < n_grp - 1:
                    sum_copy(to_g, g).start()
    for dg, ds in peers:
        row_copy(peer(dg, ds), (s, g)).wait_send()
    total = part_send[g]
    for dg in range(1, n_grp):
        from_g = lax.rem(g + dg, n_grp)
        sum_copy(from_g, from_g).wait_recv()
        total += part_recv[from_g]
    out[...] = total
    for dg in range(1, n_grp):
        sum_copy(lax.rem(g + dg, n_grp), g).wait_send()


def run_fused(n_slab, n_grp, cap, collective_id, args):
    pencils, send_map, index, frac, ori_count, spectra, class_ids, ctf = args
    ky_loc, kx_loc = pencils.shape[:2]
    rows_u = spectra.shape[1]
    slots = n_slab * CAP
    chunks = ky_loc // 4
    vmem, smem, hbm = (pl.BlockSpec(memory_space=m) for m in (pltpu.VMEM, pltpu.SMEM, pl.ANY))
    dma = pltpu.SemaphoreType.DMA
    return pl.pallas_call(
        lambda *refs: fused(n_slab, n_grp, cap, *refs),
        out_shape=[
            jax.ShapeDtypeStruct((PART_DEV, ORI_MAX * TRANS // n_grp), jnp.float32),
            jax.ShapeDtypeStruct((1,), jnp.int32),
        ],
        in_specs=[hbm] * 11,
        out_specs=[vmem, smem],
        scratch_shapes=[
            pltpu.VMEM((n_grp, 2, n_slab // 2, 1, slots), jnp.int32),
            pltpu.VMEM((chunks, 4, kx_loc, 2 * NF), jnp.float32),
            pltpu.VMEM((2 * NF, 2 * NF), jnp.bfloat16),
            pltpu.VMEM((ky_loc // 2, NF, 256), jnp.bfloat16),
            pltpu.VMEM(spectra.shape, jnp.bfloat16),
            pltpu.VMEM(ctf.shape, jnp.bfloat16),
            pltpu.VMEM((2, NF, 256), jnp.bfloat16),
            pltpu.VMEM((rows_u, 128), jnp.float32),
            pltpu.VMEM((n_grp, n_slab, slots), jnp.float32),
            pltpu.VMEM((n_grp, n_slab, slots), jnp.float32),
            pltpu.VMEM((2, 256, ky_loc // 2 * NF), jnp.bfloat16),
            pltpu.VMEM((n_grp, n_slab, cap, 128), jnp.bfloat16),
            pltpu.VMEM((n_grp, n_slab * cap, 128), jnp.bfloat16),
            pltpu.VMEM((2, PART_DEV, rows_u, NF), jnp.bfloat16),
            pltpu.VMEM((2, PART_DEV * rows_u, NF), jnp.bfloat16),
            pltpu.VMEM((n_grp, PART_DEV, 128), jnp.float32),
            pltpu.VMEM((n_grp, PART_DEV, 128), jnp.float32),
            pltpu.SMEM(class_ids.shape, jnp.int32),
            pltpu.SMEM(ori_count.shape, jnp.int32),
            pltpu.VMEM(send_map.shape[2:], jnp.int32),
            pltpu.VMEM((2, ORI_MAX, rows_u), jnp.int32),
            pltpu.VMEM((ORI_MAX, rows_u), jnp.float32),
            dma((10,)),
            dma((chunks,)),
            dma((2, n_slab // 2)),
            dma((n_slab // 2,)),
            dma((1 + n_grp,)),
            dma((1 + n_grp,)),
            dma((n_grp, n_slab)),
            dma((n_grp, n_slab)),
            dma((n_grp,)),
            dma((n_grp,)),
        ],
        compiler_params=pltpu.CompilerParams(
            collective_id=collective_id, has_side_effects=True, vmem_limit_bytes=60 * 2**20),
    )(
        class_ids, ori_count, send_map[0, 0], index[:, 0], frac[0], pencils, jnp.asarray(dft_table()),
        spectra, ctf, jnp.asarray(column_phases()), jnp.asarray(row_phases()),
    )


def listed(n_slab, n_grp, *args):
    scores, load = run_fused(n_slab, n_grp, CAP_FAST, 1, args)
    return lax.cond(
        load.reshape(()) > 0,
        lambda: run_fused(n_slab, n_grp, n_slab * CAP, 2, args)[0],
        lambda: scores,
    )


def solution(mesh):
    n_slab, n_grp = mesh.shape["slab"], mesh.shape["grp"]

    def body(*args):
        if n_slab * CAP == 128 and n_grp == 4:
            return listed(n_slab, n_grp, *args)
        return shards(*args)

    return jax.shard_map(
        body,
        mesh=mesh,
        in_specs=(
            P("slab", "grp", None),
            P("slab", "grp", None, None),
            P(None, "slab", None, "grp"),
            P("slab", None, "grp"),
            P("slab"),
            P("slab", "grp", None),
            P("slab"),
            P(None, "grp", None),
        ),
        out_specs=P("slab", "grp"),
        check_vma=False,
    )
```

```python
import math

import jax
import jax.numpy as jnp
import numpy as np
from jax import lax
from jax.experimental import pallas as pl
from jax.experimental.pallas import tpu as pltpu
from jax.sharding import PartitionSpec as P

NF = 256
CAP = 16
ORI_MAX = 8
TSIDE = 8
CLASSES = 16
PART_DEV = 8
TRANS = 64


def phase_factors(first_row, row_total):
    side_ids = jnp.arange(TSIDE, dtype=jnp.int32) - TSIDE // 2
    rows_u = first_row + jnp.arange(row_total, dtype=jnp.int32)
    cols_v = jnp.arange(NF, dtype=jnp.int32)
    turns_u = side_ids[:, None] * rows_u[None, :] % NF
    turns_v = side_ids[:, None] * cols_v[None, :] % NF
    angle_u = -2.0 * math.pi / NF * turns_u.astype(jnp.float32)
    angle_v = -2.0 * math.pi / NF * turns_v.astype(jnp.float32)
    return (jnp.cos(angle_u), jnp.sin(angle_u), jnp.cos(angle_v), jnp.sin(angle_v))


def shift_score(slice_rows, weighted, factors):
    cos_u, sin_u, cos_v, sin_v = factors
    row_total = slice_rows.shape[0]
    cu = cos_u[:, None, :, None]
    su = sin_u[:, None, :, None]
    cv = cos_v[None, :, None, :]
    sv = sin_v[None, :, None, :]
    cosines = (cu * cv - su * sv).reshape(TRANS, row_total, NF)
    sines = (su * cv + cu * sv).reshape(TRANS, row_total, NF)
    real_part = slice_rows[None, :, :NF]
    imag_part = slice_rows[None, :, NF:]
    shifted = jnp.concatenate(
        [real_part * cosines - imag_part * sines, real_part * sines + imag_part * cosines], axis=-1
    ).astype(jnp.bfloat16)
    flat_refs = shifted.reshape(TRANS, -1)
    return (
        lax.dot_general(
            weighted, flat_refs, (((1,), (1,)), ((), ())), preferred_element_type=jnp.float32
        )
        / NF
    )


def shards(pencils, send_map, interp_index, interp_frac, ori_count, spectra, class_ids, ctf_table):
    slab_depth = NF // lax.axis_size("slab")
    freq_index = jnp.arange(NF, dtype=jnp.int32)
    phase_turns = freq_index[:, None] * freq_index[None, :] % NF
    angles = 2.0 * math.pi / NF * phase_turns.astype(jnp.float32)
    cosine = jnp.cos(angles)
    sine_table = jnp.sin(angles)
    norm_scale = 1.0 / math.sqrt(NF)
    real_in = pencils[..., :NF]
    imag_in = pencils[..., NF:]
    highest = lax.Precision.HIGHEST
    real_out = (
        jnp.einsum("yxz,zk->kyx", real_in, cosine, precision=highest)
        + jnp.einsum("yxz,zk->kyx", imag_in, sine_table, precision=highest)
    ) * norm_scale
    imag_out = (
        jnp.einsum("yxz,zk->kyx", imag_in, cosine, precision=highest)
        - jnp.einsum("yxz,zk->kyx", real_in, sine_table, precision=highest)
    ) * norm_scale
    planes = jnp.stack([real_out, imag_out], axis=2).astype(jnp.bfloat16)
    slab_planes = lax.all_to_all(planes, "slab", split_axis=0, concat_axis=1, tiled=True)
    gathered = lax.all_gather(slab_planes, "grp", axis=3, tiled=True)
    row_table = gathered.reshape(slab_depth * NF, 2 * NF)
    slot_map = send_map[0, 0]
    picked = jnp.take(row_table, jnp.maximum(slot_map, 0).reshape(-1), axis=0)
    picked = picked * (slot_map >= 0).reshape(-1, 1).astype(jnp.bfloat16)
    outgoing = picked.reshape(slot_map.shape[0], CAP, 2 * NF)
    arrived = lax.all_to_all(outgoing, "slab", split_axis=0, concat_axis=0, tiled=True)
    buffer = arrived.reshape(-1, 2 * NF)
    rows_local = interp_frac.shape[2]
    tap_index = interp_index[:, 0]
    weights_tap = interp_frac[0][..., None]
    lower_rows = jnp.take(buffer, tap_index[0].reshape(-1), axis=0).reshape(
        ORI_MAX, rows_local, 2 * NF
    )
    upper_rows = jnp.take(buffer, tap_index[1].reshape(-1), axis=0).reshape(
        ORI_MAX, rows_local, 2 * NF
    )
    slices = (1.0 - weights_tap) * lower_rows.astype(jnp.float32) + weights_tap * upper_rows.astype(
        jnp.float32
    )
    onehot = (class_ids[:, None] == jnp.arange(CLASSES, dtype=jnp.int32)[None, :]).astype(
        jnp.bfloat16
    )
    ctf_rows = jnp.dot(
        onehot, ctf_table.reshape(CLASSES, -1), preferred_element_type=jnp.float32
    ).reshape(PART_DEV, rows_local, NF)
    weighted = (
        (jnp.concatenate([ctf_rows, ctf_rows], axis=-1) * spectra.astype(jnp.float32))
        .astype(jnp.bfloat16)
        .reshape(PART_DEV, -1)
    )
    first_row = lax.axis_index("grp") * rows_local
    factors = phase_factors(first_row, rows_local)
    live_count = ori_count[0]

    def orient_score(orient):
        result = shift_score(slices[orient], weighted, factors)
        return jnp.where(orient < live_count, result, jnp.zeros_like(result))

    blocks_out = lax.map(orient_score, jnp.arange(ORI_MAX, dtype=jnp.int32))
    partial_scores = jnp.transpose(blocks_out, (1, 0, 2)).reshape(PART_DEV, ORI_MAX * TRANS)
    return lax.psum_scatter(partial_scores, "grp", scatter_dimension=1, tiled=True)


MESH = pl.DeviceIdType.MESH
CAP_FAST = 32


def dft_table():
    turns = np.outer(np.arange(NF), np.arange(NF)) % NF
    angle = 2.0 * np.pi / NF * turns
    cos, sin = np.cos(angle) / math.sqrt(NF), np.sin(angle) / math.sqrt(NF)
    return np.block([[cos, sin], [-sin, cos]]).astype(jnp.bfloat16)


def column_phases():
    side = np.arange(TSIDE) - TSIDE // 2
    angle = 2.0 * np.pi / NF * (np.outer(np.arange(NF), side) % NF)
    cos, sin = np.tile(np.cos(angle), (1, TSIDE)), np.tile(np.sin(angle), (1, TSIDE))
    full = np.block([[cos, -sin], [sin, cos]]).astype(np.float32)
    high = full.astype(jnp.bfloat16)
    low = (full - high.astype(np.float32)).astype(jnp.bfloat16)
    both = np.concatenate([high, low], axis=1).reshape(2, 2, 128, 256)
    return both.transpose(1, 0, 2, 3).reshape(2, NF, 256)


def row_phases():
    side = np.arange(TSIDE) - TSIDE // 2
    angle = 2.0 * np.pi / NF * (np.outer(np.arange(NF), side) % NF)
    cos, sin = np.repeat(np.cos(angle), TSIDE, 1), np.repeat(np.sin(angle), TSIDE, 1)
    return np.concatenate([cos, sin], axis=1).astype(np.float32)


def iota(shape, axis):
    return lax.broadcasted_iota(jnp.int32, shape, axis)


def fused(
    n_slab, n_grp, cap,
    class_hbm, map_hbm, index_hbm, frac_hbm, pencils, dft, spectra, ctf, phase_v, phase_u,
    out, load_out, orient_out,
    maps, lines, table_w, planes, spec_in, ctf_in, col_ph, row_ph, rank_ref, key_ref, picked2, sendbuf,
    recv, weighted, product, part_send, part_recv, class_ids, send_map, index, frac,
    load_sem, line_sem, map_send, map_recv, row_send, row_recv, sum_send, sum_recv,
):
    s, g = lax.axis_index("slab"), lax.axis_index("grp")
    ky_loc, kx_loc = pencils.shape[0], pencils.shape[1]
    rows_u = spectra.shape[1]
    slots = n_slab * CAP
    chunks = lines.shape[0]
    step = ky_loc // chunks
    peers = [(dg, ds) for dg in range(n_grp) for ds in range(n_slab) if dg + ds > 0]

    x, core = g // 2, g % 2
    order = [(1 - x) * 2 + core, (1 - x) * 2 + 1 - core, x * 2 + 1 - core, g]

    def peer(dg, ds):
        return lax.rem(s + ds, n_slab), lax.rem(g + dg, n_grp)

    barrier = pltpu.get_barrier_semaphore()
    for dg, ds in peers:
        pl.semaphore_signal(barrier, inc=1, device_id=peer(dg, ds), device_id_type=MESH)
    loads = [
        pltpu.make_async_copy(a, b, load_sem.at[i])
        for i, (a, b) in enumerate(
            [(map_hbm, send_map), (dft, table_w), (class_hbm, class_ids),
             (index_hbm, index), (frac_hbm, frac), (ctf, ctf_in), (spectra, spec_in), (phase_v, col_ph),
             (phase_u.at[pl.ds(pl.multiple_of(g * rows_u, rows_u), rows_u)], row_ph)]
        )
    ]

    def line_load(c):
        return pltpu.make_async_copy(pencils.at[pl.ds(c * step, step)], lines.at[c], line_sem.at[c])

    for copy in loads[:2]:
        copy.start()
    for c in range(chunks):
        line_load(c).start()
    for copy in loads[2:]:
        copy.start()

    def transform(c, carry):
        line_load(c).wait()
        block = lines[c].reshape(step * kx_loc, 2 * NF).astype(jnp.bfloat16)
        lanes = lax.dot_general(
            table_w[...], block, (((1,), (1,)), ((), ())), preferred_element_type=jnp.float32
        ).astype(jnp.bfloat16)
        for h in range(step // 2):
            planes[c * (step // 2) + h, :, :128] = lanes[:NF, h * 128:(h + 1) * 128]
            planes[c * (step // 2) + h, :, 128:] = lanes[NF:, h * 128:(h + 1) * 128]
        return carry

    loads[1].wait()
    for c in range(chunks // 4):
        transform(c, 0)
    loads[0].wait()
    maps[g, s] = jnp.concatenate([send_map[...]] * n_slab, axis=1)
    pl.semaphore_wait(barrier, len(peers))

    def map_copy(to, whose):
        return pltpu.make_async_remote_copy(
            src_ref=maps.at[g, s], dst_ref=maps.at[whose[1], whose[0]],
            send_sem=map_send.at[to[0], to[1]], recv_sem=map_recv.at[whose[0], whose[1]],
            device_id=to, device_id_type=MESH)

    for dg, ds in peers:
        map_copy(peer(dg, ds), (s, g)).start()

    for c in range(chunks // 4, chunks):
        transform(c, 0)

    for dg, ds in peers:
        whose = peer(dg, ds)
        map_copy(whose, whose).wait_recv()

    lane = iota((n_slab, slots), 1)
    rows = jnp.concatenate(
        [sum(jnp.where(lane // CAP == a, maps[b, a], 0) for a in range(n_slab)) for b in range(n_grp)],
        axis=0,
    )
    shift = ky_loc.bit_length() - 1
    used = rows >= 0
    ky = rows & (NF - 1)
    home = jnp.where(used, ky >> shift, -1)
    tri = (iota((slots, slots), 0) < iota((slots, slots), 1)).astype(jnp.float32).astype(jnp.bfloat16)

    def ranks(mask):
        ones = jnp.where(mask, 1.0, 0.0)
        return jnp.dot(ones.astype(jnp.bfloat16), tri, preferred_element_type=jnp.float32), ones

    mine = home == s
    rank, _ = ranks(mine)
    rank = jnp.where(mine, rank, -1.0)
    ky_own = ky & (ky_loc - 1)
    kz = (iota(rows.shape, 1) // CAP) * (NF // n_slab) + (rows >> 8)
    code = (((ky_own >> 1) * NF + kz) * 2 + (ky_own & 1) + 1).astype(jnp.float32)
    for b in range(n_grp):
        rank_ref[b] = rank[b * n_slab:(b + 1) * n_slab]
        key_ref[b] = code[b * n_slab:(b + 1) * n_slab]
    def row_copy(to, whose):
        return pltpu.make_async_remote_copy(
            src_ref=sendbuf.at[to[1], to[0]],
            dst_ref=recv.at[whose[1], pl.ds(pl.multiple_of(whose[0] * cap, cap), cap)],
            send_sem=row_send.at[to[1], to[0]], recv_sem=row_recv.at[whose[1], whose[0]],
            device_id=to, device_id_type=MESH)

    pairs = ky_loc // 2
    at_once = 256 // cap
    lane256 = iota((256, NF), 1)
    lane128 = iota((256, 128), 1)

    def pick(i):
        to_g = order[i]
        picked = picked2.at[i % 2]
        for q in range(n_slab // at_once):
            rk = rank_ref[to_g, q * at_once:(q + 1) * at_once]
            cd = key_ref[to_g, q * at_once:(q + 1) * at_once]
            places = iota((at_once, cap, slots), 1).astype(jnp.float32)
            hit = jnp.where(rk[:, None, :] == places, cd[:, None, :], 0.0)
            found = (jnp.sum(hit, axis=2, keepdims=True) - 1.0).reshape(256, 1).astype(jnp.int32)
            odd = (found & 1) == 1
            pair = jnp.broadcast_to((found >> (NF.bit_length())).astype(jnp.float32), (256, NF)).astype(jnp.bfloat16)
            plane_hit = jnp.where(((found >> 1) & (NF - 1)) == lane256, 1.0, 0.0).astype(jnp.bfloat16)
            for j in range(pairs):
                picked[:, j * NF:(j + 1) * NF] = jnp.where(
                    pair == jnp.bfloat16(j), plane_hit, jnp.bfloat16(0))
            got = jnp.dot(picked[...], planes[...].reshape(pairs * NF, 256),
                          preferred_element_type=jnp.float32)
            a, b = got[:, :128], got[:, 128:]
            row = jnp.where(lane128 < 64, jnp.where(odd, pltpu.roll(a, 64, 1), a),
                            jnp.where(odd, b, pltpu.roll(b, 64, 1)))
            sendbuf[to_g, q * at_once:(q + 1) * at_once] = row.astype(jnp.bfloat16).reshape(at_once, cap, 128)
        for ds in sorted(range(n_slab), key=lambda d: -min(d, n_slab - d)):
            if i < n_grp - 1 or ds > 0:
                row_copy((lax.rem(s + ds, n_slab), to_g), (s, g)).start()

    for i in range(n_grp):
        pick(i)
    recv[g, pl.ds(pl.multiple_of(s * cap, cap), cap)] = sendbuf[g, s]

    most = jnp.zeros((rows.shape[0], 1), jnp.float32)
    for a in range(n_slab):
        most = jnp.maximum(most, jnp.sum(jnp.where(home == a, 1.0, 0.0), axis=1, keepdims=True))
    load_out[0] = (jnp.max(most) > cap).astype(jnp.int32)

    for copy in loads[2:]:
        copy.wait()
    for p in range(PART_DEV):
        for h in range(2):
            ctf_rows = ctf_in[class_ids[p], :, h * 128:(h + 1) * 128].astype(jnp.float32)
            for part in range(2):
                at = part * NF + h * 128
                weighted[h, p, :, part * 128:(part + 1) * 128] = (
                    ctf_rows * spec_in[p, :, at:at + 128].astype(jnp.float32)
                ).astype(jnp.bfloat16)

    own = jnp.sum(jnp.where(lane // CAP == iota((n_slab, slots), 0), maps_row(maps, s, g, n_slab), 0),
                  axis=0, keepdims=True)
    own_home = jnp.where(own >= 0, (own & (NF - 1)) >> shift, -1)
    from_a = own_home == iota((n_slab, slots), 0)
    own_rank, ones = ranks(from_a)
    base = (iota((n_slab, slots), 0) * cap).astype(jnp.float32)
    place = jnp.sum(ones * (own_rank + base + 1.0), axis=0, keepdims=True) - 1.0
    spread = jnp.where(place == iota((n_slab * cap, slots), 0).astype(jnp.float32), 1.0, 0.0).astype(jnp.bfloat16)

    for dg, ds in peers:
        map_copy(peer(dg, ds), (s, g)).wait_send()
    lane_s = iota((slots, 128), 1)

    def lists(half, turn):
        got = []
        for b in range(2):
            from_g = half * 2 + b
            got.append(lax.dot_general(spread, recv[from_g], (((0,), (0,)), ((), ())),
                                       preferred_element_type=jnp.float32))
        a, b = got
        block = jnp.concatenate([jnp.where(lane_s < 64, a, pltpu.roll(b, 64, 1)),
                                 jnp.where(lane_s < 64, pltpu.roll(a, 64, 1), b)], axis=1)
        block = block.astype(jnp.bfloat16)
        return jnp.concatenate([block, block], axis=0)

    def sum_copy(to_g, whose_g):
        return pltpu.make_async_remote_copy(
            src_ref=part_send.at[to_g], dst_ref=part_recv.at[whose_g],
            send_sem=sum_send.at[to_g], recv_sem=sum_recv.at[whose_g],
            device_id=(s, to_g), device_id_type=MESH)

    slot_id = iota((slots, rows_u), 0)
    lane_p = iota((PART_DEV, 128), 1)

    def half_score(o, half, received, buf):
        i0 = index[0, pl.ds(o, 1), :]
        i1 = index[1, pl.ds(o, 1), :]
        w = frac[pl.ds(o, 1), :]
        taps = jnp.where(slot_id == i0, 1.0 - w, 0.0) + jnp.where(slot_id == i1, w, 0.0)
        high = taps.astype(jnp.bfloat16)
        low = (taps - high.astype(jnp.float32)).astype(jnp.bfloat16)
        rows_o = lax.dot_general(
            jnp.concatenate([high, low], axis=0), received, (((0,), (0,)), ((), ())),
            preferred_element_type=jnp.float32)
        sr, si = rows_o[:, :128], rows_o[:, 128:]
        for p in range(PART_DEV):
            wr = weighted[half, p, :, :128].astype(jnp.float32)
            wi = weighted[half, p, :, 128:].astype(jnp.float32)
            product[buf, p * rows_u:(p + 1) * rows_u, :128] = (wr * sr + wi * si).astype(jnp.bfloat16)
            product[buf, p * rows_u:(p + 1) * rows_u, 128:] = (wr * si - wi * sr).astype(jnp.bfloat16)
        z = jnp.dot(product[buf], col_ph[half], preferred_element_type=jnp.float32)
        z = (z[:, :128] + z[:, 128:]).reshape(PART_DEV, rows_u, 128)
        return jnp.sum(z * row_ph[...][None], axis=1)

    partial = {}
    for turn, half in enumerate([1 - x, x]):
        for i in (0, 1) if turn == 0 else (2, 3):
            for ds in range(n_slab):
                if i < n_grp - 1 or ds > 0:
                    whose = (lax.rem(s + ds, n_slab), order[i])
                    row_copy(whose, whose).wait_recv()
        received = lists(half, turn)
        for i in range(n_grp):
            to_g = order[i]
            folded = []
            for e in range(2):
                o = to_g * 2 + e
                t = half_score(o, half, received, e)
                if turn == 0:
                    partial[i, e] = t
                else:
                    t = partial[i, e] + t
                    t = (t + pltpu.roll(t, 64, 1)) * (1.0 / NF)
                    folded.append(t)
            if turn == 1:
                part_send[to_g] = jnp.where(lane_p < 64, folded[0], folded[1])
                if i < n_grp - 1:
                    sum_copy(to_g, g).start()
    for dg, ds in peers:
        row_copy(peer(dg, ds), (s, g)).wait_send()
    total = part_send[g]
    for dg in range(1, n_grp):
        from_g = lax.rem(g + dg, n_grp)
        sum_copy(from_g, from_g).wait_recv()
        total += part_recv[from_g]
    out[...] = total
    orient_out[...] = g * (ORI_MAX // n_grp) + lane_p // TRANS
    for dg in range(1, n_grp):
        sum_copy(lax.rem(g + dg, n_grp), g).wait_send()


def maps_row(maps, s, g, n_slab):
    return jnp.concatenate([maps[g, a, pl.ds(s, 1), :] for a in range(n_slab)], axis=0)


def run_fused(n_slab, n_grp, cap, collective_id, args):
    pencils, send_map, index, frac, _, spectra, class_ids, ctf = args
    ky_loc, kx_loc = pencils.shape[:2]
    rows_u = spectra.shape[1]
    slots = n_slab * CAP
    chunks = ky_loc // 4
    vmem, smem = (pl.BlockSpec(memory_space=m) for m in (pltpu.VMEM, pltpu.SMEM))
    dma = pltpu.SemaphoreType.DMA
    return pl.pallas_call(
        lambda *refs: fused(n_slab, n_grp, cap, *refs),
        out_shape=[
            jax.ShapeDtypeStruct((PART_DEV, ORI_MAX * TRANS // n_grp), jnp.float32),
            jax.ShapeDtypeStruct((1,), jnp.int32),
            jax.ShapeDtypeStruct((PART_DEV, ORI_MAX * TRANS // n_grp), jnp.int32),
        ],
        in_specs=[pl.BlockSpec(memory_space=pltpu.HBM)] * 10,
        out_specs=[vmem, smem, vmem],
        scratch_shapes=[
            pltpu.VMEM((n_grp, n_slab, n_slab, slots), jnp.int32),
            pltpu.VMEM((chunks, 4, kx_loc, 2 * NF), jnp.float32),
            pltpu.VMEM((2 * NF, 2 * NF), jnp.bfloat16),
            pltpu.VMEM((ky_loc // 2, NF, 256), jnp.bfloat16),
            pltpu.VMEM(spectra.shape, jnp.bfloat16),
            pltpu.VMEM(ctf.shape, jnp.bfloat16),
            pltpu.VMEM((2, NF, 256), jnp.bfloat16),
            pltpu.VMEM((rows_u, 128), jnp.float32),
            pltpu.VMEM((n_grp, n_slab, slots), jnp.float32),
            pltpu.VMEM((n_grp, n_slab, slots), jnp.float32),
            pltpu.VMEM((2, 256, ky_loc // 2 * NF), jnp.bfloat16),
            pltpu.VMEM((n_grp, n_slab, cap, 128), jnp.bfloat16),
            pltpu.VMEM((n_grp, n_slab * cap, 128), jnp.bfloat16),
            pltpu.VMEM((2, PART_DEV, rows_u, NF), jnp.bfloat16),
            pltpu.VMEM((2, PART_DEV * rows_u, NF), jnp.bfloat16),
            pltpu.VMEM((n_grp, PART_DEV, 128), jnp.float32),
            pltpu.VMEM((n_grp, PART_DEV, 128), jnp.float32),
            pltpu.SMEM(class_ids.shape, jnp.int32),
            pltpu.VMEM(send_map.shape[2:], jnp.int32),
            pltpu.VMEM((2, ORI_MAX, rows_u), jnp.int32),
            pltpu.VMEM((ORI_MAX, rows_u), jnp.float32),
            dma((9,)),
            dma((chunks,)),
            dma((n_slab, n_grp)),
            dma((n_slab, n_grp)),
            dma((n_grp, n_slab)),
            dma((n_grp, n_slab)),
            dma((n_grp,)),
            dma((n_grp,)),
        ],
        compiler_params=pltpu.CompilerParams(
            collective_id=collective_id, has_side_effects=True, vmem_limit_bytes=60 * 2**20),
    )(
        class_ids, send_map[0, 0], index[:, 0], frac[0], pencils, jnp.asarray(dft_table()),
        spectra, ctf, jnp.asarray(column_phases()), jnp.asarray(row_phases()),
    )


def listed(n_slab, n_grp, *args):
    scores, load, orient = run_fused(n_slab, n_grp, CAP_FAST, 1, args)
    chosen = lax.cond(
        load.reshape(()) > 0,
        lambda: run_fused(n_slab, n_grp, n_slab * CAP, 2, args)[0],
        lambda: scores,
    )
    return jnp.where(orient < args[4][0], chosen, 0.0)


def solution(mesh):
    n_slab, n_grp = mesh.shape["slab"], mesh.shape["grp"]

    def body(*args):
        if n_slab * CAP == 128 and n_grp == 4:
            return listed(n_slab, n_grp, *args)
        return shards(*args)

    return jax.shard_map(
        body,
        mesh=mesh,
        in_specs=(
            P("slab", "grp", None),
            P("slab", "grp", None, None),
            P(None, "slab", None, "grp"),
            P("slab", None, "grp"),
            P("slab"),
            P("slab", "grp", None),
            P("slab"),
            P(None, "grp", None),
        ),
        out_specs=P("slab", "grp"),
        check_vma=False,
    )
```

```python
import math

import jax
import jax.numpy as jnp
import numpy as np
from jax import lax
from jax.experimental import pallas as pl
from jax.experimental.pallas import tpu as pltpu
from jax.sharding import PartitionSpec as P

NF = 256
CAP = 16
ORI_MAX = 8
TSIDE = 8
CLASSES = 16
PART_DEV = 8
TRANS = 64


def phase_factors(first_row, row_total):
    side_ids = jnp.arange(TSIDE, dtype=jnp.int32) - TSIDE // 2
    rows_u = first_row + jnp.arange(row_total, dtype=jnp.int32)
    cols_v = jnp.arange(NF, dtype=jnp.int32)
    turns_u = side_ids[:, None] * rows_u[None, :] % NF
    turns_v = side_ids[:, None] * cols_v[None, :] % NF
    angle_u = -2.0 * math.pi / NF * turns_u.astype(jnp.float32)
    angle_v = -2.0 * math.pi / NF * turns_v.astype(jnp.float32)
    return (jnp.cos(angle_u), jnp.sin(angle_u), jnp.cos(angle_v), jnp.sin(angle_v))


def shift_score(slice_rows, weighted, factors):
    cos_u, sin_u, cos_v, sin_v = factors
    row_total = slice_rows.shape[0]
    cu = cos_u[:, None, :, None]
    su = sin_u[:, None, :, None]
    cv = cos_v[None, :, None, :]
    sv = sin_v[None, :, None, :]
    cosines = (cu * cv - su * sv).reshape(TRANS, row_total, NF)
    sines = (su * cv + cu * sv).reshape(TRANS, row_total, NF)
    real_part = slice_rows[None, :, :NF]
    imag_part = slice_rows[None, :, NF:]
    shifted = jnp.concatenate(
        [real_part * cosines - imag_part * sines, real_part * sines + imag_part * cosines], axis=-1
    ).astype(jnp.bfloat16)
    flat_refs = shifted.reshape(TRANS, -1)
    return (
        lax.dot_general(
            weighted, flat_refs, (((1,), (1,)), ((), ())), preferred_element_type=jnp.float32
        )
        / NF
    )


def shards(pencils, send_map, interp_index, interp_frac, ori_count, spectra, class_ids, ctf_table):
    slab_depth = NF // lax.axis_size("slab")
    freq_index = jnp.arange(NF, dtype=jnp.int32)
    phase_turns = freq_index[:, None] * freq_index[None, :] % NF
    angles = 2.0 * math.pi / NF * phase_turns.astype(jnp.float32)
    cosine = jnp.cos(angles)
    sine_table = jnp.sin(angles)
    norm_scale = 1.0 / math.sqrt(NF)
    real_in = pencils[..., :NF]
    imag_in = pencils[..., NF:]
    highest = lax.Precision.HIGHEST
    real_out = (
        jnp.einsum("yxz,zk->kyx", real_in, cosine, precision=highest)
        + jnp.einsum("yxz,zk->kyx", imag_in, sine_table, precision=highest)
    ) * norm_scale
    imag_out = (
        jnp.einsum("yxz,zk->kyx", imag_in, cosine, precision=highest)
        - jnp.einsum("yxz,zk->kyx", real_in, sine_table, precision=highest)
    ) * norm_scale
    planes = jnp.stack([real_out, imag_out], axis=2).astype(jnp.bfloat16)
    slab_planes = lax.all_to_all(planes, "slab", split_axis=0, concat_axis=1, tiled=True)
    gathered = lax.all_gather(slab_planes, "grp", axis=3, tiled=True)
    row_table = gathered.reshape(slab_depth * NF, 2 * NF)
    slot_map = send_map[0, 0]
    picked = jnp.take(row_table, jnp.maximum(slot_map, 0).reshape(-1), axis=0)
    picked = picked * (slot_map >= 0).reshape(-1, 1).astype(jnp.bfloat16)
    outgoing = picked.reshape(slot_map.shape[0], CAP, 2 * NF)
    arrived = lax.all_to_all(outgoing, "slab", split_axis=0, concat_axis=0, tiled=True)
    buffer = arrived.reshape(-1, 2 * NF)
    rows_local = interp_frac.shape[2]
    tap_index = interp_index[:, 0]
    weights_tap = interp_frac[0][..., None]
    lower_rows = jnp.take(buffer, tap_index[0].reshape(-1), axis=0).reshape(
        ORI_MAX, rows_local, 2 * NF
    )
    upper_rows = jnp.take(buffer, tap_index[1].reshape(-1), axis=0).reshape(
        ORI_MAX, rows_local, 2 * NF
    )
    slices = (1.0 - weights_tap) * lower_rows.astype(jnp.float32) + weights_tap * upper_rows.astype(
        jnp.float32
    )
    onehot = (class_ids[:, None] == jnp.arange(CLASSES, dtype=jnp.int32)[None, :]).astype(
        jnp.bfloat16
    )
    ctf_rows = jnp.dot(
        onehot, ctf_table.reshape(CLASSES, -1), preferred_element_type=jnp.float32
    ).reshape(PART_DEV, rows_local, NF)
    weighted = (
        (jnp.concatenate([ctf_rows, ctf_rows], axis=-1) * spectra.astype(jnp.float32))
        .astype(jnp.bfloat16)
        .reshape(PART_DEV, -1)
    )
    first_row = lax.axis_index("grp") * rows_local
    factors = phase_factors(first_row, rows_local)
    live_count = ori_count[0]

    def orient_score(orient):
        result = shift_score(slices[orient], weighted, factors)
        return jnp.where(orient < live_count, result, jnp.zeros_like(result))

    blocks_out = lax.map(orient_score, jnp.arange(ORI_MAX, dtype=jnp.int32))
    partial_scores = jnp.transpose(blocks_out, (1, 0, 2)).reshape(PART_DEV, ORI_MAX * TRANS)
    return lax.psum_scatter(partial_scores, "grp", scatter_dimension=1, tiled=True)


MESH = pl.DeviceIdType.MESH
CAP_FAST = 32


def dft_table():
    turns = np.outer(np.arange(NF), np.arange(NF)) % NF
    angle = 2.0 * np.pi / NF * turns
    cos, sin = np.cos(angle) / math.sqrt(NF), np.sin(angle) / math.sqrt(NF)
    return np.block([[cos, sin], [-sin, cos]]).astype(jnp.bfloat16)


def column_phases():
    side = np.arange(TSIDE) - TSIDE // 2
    angle = 2.0 * np.pi / NF * (np.outer(np.arange(NF), side) % NF)
    cos, sin = np.tile(np.cos(angle), (1, TSIDE)), np.tile(np.sin(angle), (1, TSIDE))
    full = np.block([[cos, -sin], [sin, cos]]).astype(np.float32)
    high = full.astype(jnp.bfloat16)
    low = (full - high.astype(np.float32)).astype(jnp.bfloat16)
    both = np.concatenate([high, low], axis=1).reshape(2, 2, 128, 256)
    return both.transpose(1, 0, 2, 3).reshape(2, NF, 256)


def row_phases():
    side = np.arange(TSIDE) - TSIDE // 2
    angle = 2.0 * np.pi / NF * (np.outer(np.arange(NF), side) % NF)
    cos, sin = np.repeat(np.cos(angle), TSIDE, 1), np.repeat(np.sin(angle), TSIDE, 1)
    return np.concatenate([cos, sin], axis=1).astype(np.float32)


def iota(shape, axis):
    return lax.broadcasted_iota(jnp.int32, shape, axis)


def fused(
    n_slab, n_grp, cap,
    class_hbm, count_hbm, map_hbm, index_hbm, frac_hbm, pencils, dft, spectra, ctf, phase_v, phase_u,
    out, load_out, listed_out,
    maps, lines, table_w, planes, spec_in, ctf_in, col_ph, row_ph, rank_ref, key_ref, picked2, sendbuf,
    recv, weighted, product, part_send, part_recv, class_ids, ori_count, send_map, index, frac,
    load_sem, line_sem, map_send, map_recv, row_send, row_recv, sum_send, sum_recv,
):
    s, g = lax.axis_index("slab"), lax.axis_index("grp")
    ky_loc, kx_loc = pencils.shape[0], pencils.shape[1]
    rows_u = spectra.shape[1]
    slots = n_slab * CAP
    chunks = lines.shape[0]
    step = ky_loc // chunks
    peers = [(dg, ds) for dg in range(n_grp) for ds in range(n_slab) if dg + ds > 0]

    x, core = g // 2, g % 2
    order = [(1 - x) * 2 + core, (1 - x) * 2 + 1 - core, x * 2 + 1 - core, g]

    def peer(dg, ds):
        return lax.rem(s + ds, n_slab), lax.rem(g + dg, n_grp)

    barrier = pltpu.get_barrier_semaphore()
    for dg, ds in peers:
        pl.semaphore_signal(barrier, inc=1, device_id=peer(dg, ds), device_id_type=MESH)
    loads = [
        pltpu.make_async_copy(a, b, load_sem.at[i])
        for i, (a, b) in enumerate(
            [(map_hbm, send_map), (dft, table_w), (class_hbm, class_ids), (count_hbm, ori_count),
             (index_hbm, index), (frac_hbm, frac), (ctf, ctf_in), (spectra, spec_in), (phase_v, col_ph),
             (phase_u.at[pl.ds(pl.multiple_of(g * rows_u, rows_u), rows_u)], row_ph)]
        )
    ]

    def line_load(c):
        return pltpu.make_async_copy(pencils.at[pl.ds(c * step, step)], lines.at[c], line_sem.at[c])

    for copy in loads[:2]:
        copy.start()
    for c in range(chunks):
        line_load(c).start()
    for copy in loads[2:]:
        copy.start()

    def transform(c, carry):
        line_load(c).wait()
        block = lines[c].reshape(step * kx_loc, 2 * NF).astype(jnp.bfloat16)
        lanes = lax.dot_general(
            table_w[...], block, (((1,), (1,)), ((), ())), preferred_element_type=jnp.float32
        ).astype(jnp.bfloat16)
        for h in range(step // 2):
            planes[c * (step // 2) + h, :, :128] = lanes[:NF, h * 128:(h + 1) * 128]
            planes[c * (step // 2) + h, :, 128:] = lanes[NF:, h * 128:(h + 1) * 128]
        return carry

    loads[1].wait()
    for c in range(chunks // 4):
        transform(c, 0)
    loads[0].wait()
    maps[g, s] = jnp.concatenate([send_map[...]] * n_slab, axis=1)
    pl.semaphore_wait(barrier, len(peers))

    def map_copy(to, whose):
        return pltpu.make_async_remote_copy(
            src_ref=maps.at[g, s], dst_ref=maps.at[whose[1], whose[0]],
            send_sem=map_send.at[to[0], to[1]], recv_sem=map_recv.at[whose[0], whose[1]],
            device_id=to, device_id_type=MESH)

    for dg, ds in peers:
        map_copy(peer(dg, ds), (s, g)).start()

    for c in range(chunks // 4, chunks):
        transform(c, 0)

    for dg, ds in peers:
        whose = peer(dg, ds)
        map_copy(whose, whose).wait_recv()

    lane = iota((n_slab, slots), 1)
    rows = jnp.concatenate(
        [sum(jnp.where(lane // CAP == a, maps[b, a], 0) for a in range(n_slab)) for b in range(n_grp)],
        axis=0,
    )
    shift = ky_loc.bit_length() - 1
    used = rows >= 0
    ky = rows & (NF - 1)
    home = jnp.where(used, ky >> shift, -1)
    tri = (iota((slots, slots), 0) < iota((slots, slots), 1)).astype(jnp.float32).astype(jnp.bfloat16)

    def ranks(mask):
        ones = jnp.where(mask, 1.0, 0.0)
        return jnp.dot(ones.astype(jnp.bfloat16), tri, preferred_element_type=jnp.float32), ones

    mine = home == s
    rank, _ = ranks(mine)
    rank = jnp.where(mine, rank, -1.0)
    ky_own = ky & (ky_loc - 1)
    kz = (iota(rows.shape, 1) // CAP) * (NF // n_slab) + (rows >> 8)
    code = (((ky_own >> 1) * NF + kz) * 2 + (ky_own & 1) + 1).astype(jnp.float32)
    for b in range(n_grp):
        rank_ref[b] = rank[b * n_slab:(b + 1) * n_slab]
        key_ref[b] = code[b * n_slab:(b + 1) * n_slab]
    def row_copy(to, whose):
        return pltpu.make_async_remote_copy(
            src_ref=sendbuf.at[to[1], to[0]],
            dst_ref=recv.at[whose[1], pl.ds(pl.multiple_of(whose[0] * cap, cap), cap)],
            send_sem=row_send.at[to[1], to[0]], recv_sem=row_recv.at[whose[1], whose[0]],
            device_id=to, device_id_type=MESH)

    pairs = ky_loc // 2
    at_once = 256 // cap
    lane256 = iota((256, NF), 1)
    lane128 = iota((256, 128), 1)

    def pick(i):
        to_g = order[i]
        picked = picked2.at[i % 2]
        for q in range(n_slab // at_once):
            rk = rank_ref[to_g, q * at_once:(q + 1) * at_once]
            cd = key_ref[to_g, q * at_once:(q + 1) * at_once]
            places = iota((at_once, cap, slots), 1).astype(jnp.float32)
            hit = jnp.where(rk[:, None, :] == places, cd[:, None, :], 0.0)
            found = (jnp.sum(hit, axis=2, keepdims=True) - 1.0).reshape(256, 1).astype(jnp.int32)
            odd = (found & 1) == 1
            pair = jnp.broadcast_to((found >> (NF.bit_length())).astype(jnp.float32), (256, NF)).astype(jnp.bfloat16)
            plane_hit = jnp.where(((found >> 1) & (NF - 1)) == lane256, 1.0, 0.0).astype(jnp.bfloat16)
            for j in range(pairs):
                picked[:, j * NF:(j + 1) * NF] = jnp.where(
                    pair == jnp.bfloat16(j), plane_hit, jnp.bfloat16(0))
            got = jnp.dot(picked[...], planes[...].reshape(pairs * NF, 256),
                          preferred_element_type=jnp.float32)
            a, b = got[:, :128], got[:, 128:]
            row = jnp.where(lane128 < 64, jnp.where(odd, pltpu.roll(a, 64, 1), a),
                            jnp.where(odd, b, pltpu.roll(b, 64, 1)))
            sendbuf[to_g, q * at_once:(q + 1) * at_once] = row.astype(jnp.bfloat16).reshape(at_once, cap, 128)
        for ds in sorted(range(n_slab), key=lambda d: -min(d, n_slab - d)):
            if i < n_grp - 1 or ds > 0:
                row_copy((lax.rem(s + ds, n_slab), to_g), (s, g)).start()

    for i in range(n_grp):
        pick(i)
    recv[g, pl.ds(pl.multiple_of(s * cap, cap), cap)] = sendbuf[g, s]

    most = jnp.zeros((rows.shape[0], 1), jnp.float32)
    for a in range(n_slab):
        most = jnp.maximum(most, jnp.sum(jnp.where(home == a, 1.0, 0.0), axis=1, keepdims=True))
    load_out[0] = (jnp.max(most) > cap).astype(jnp.int32)

    for copy in loads[2:]:
        copy.wait()
    for p in range(PART_DEV):
        for h in range(2):
            ctf_rows = ctf_in[class_ids[p], :, h * 128:(h + 1) * 128].astype(jnp.float32)
            for part in range(2):
                at = part * NF + h * 128
                weighted[h, p, :, part * 128:(part + 1) * 128] = (
                    ctf_rows * spec_in[p, :, at:at + 128].astype(jnp.float32)
                ).astype(jnp.bfloat16)

    own = jnp.sum(jnp.where(lane // CAP == iota((n_slab, slots), 0), maps_row(maps, s, g, n_slab), 0),
                  axis=0, keepdims=True)
    own_home = jnp.where(own >= 0, (own & (NF - 1)) >> shift, -1)
    from_a = own_home == iota((n_slab, slots), 0)
    own_rank, ones = ranks(from_a)
    base = (iota((n_slab, slots), 0) * cap).astype(jnp.float32)
    place = jnp.sum(ones * (own_rank + base + 1.0), axis=0, keepdims=True) - 1.0
    spread = jnp.where(place == iota((n_slab * cap, slots), 0).astype(jnp.float32), 1.0, 0.0).astype(jnp.bfloat16)

    for dg, ds in peers:
        map_copy(peer(dg, ds), (s, g)).wait_send()
    lane_s = iota((slots, 128), 1)

    def lists(half, turn):
        got = []
        for b in range(2):
            from_g = half * 2 + b
            got.append(lax.dot_general(spread, recv[from_g], (((0,), (0,)), ((), ())),
                                       preferred_element_type=jnp.float32))
        a, b = got
        block = jnp.concatenate([jnp.where(lane_s < 64, a, pltpu.roll(b, 64, 1)),
                                 jnp.where(lane_s < 64, pltpu.roll(a, 64, 1), b)], axis=1)
        block = block.astype(jnp.bfloat16)
        return jnp.concatenate([block, block], axis=0)

    def sum_copy(to_g, whose_g):
        return pltpu.make_async_remote_copy(
            src_ref=part_send.at[to_g], dst_ref=part_recv.at[whose_g],
            send_sem=sum_send.at[to_g], recv_sem=sum_recv.at[whose_g],
            device_id=(s, to_g), device_id_type=MESH)

    slot_id = iota((slots, rows_u), 0)
    lane_p = iota((PART_DEV, 128), 1)

    def half_score(o, half, received, buf):
        i0 = index[0, pl.ds(o, 1), :]
        i1 = index[1, pl.ds(o, 1), :]
        w = frac[pl.ds(o, 1), :]
        taps = jnp.where(slot_id == i0, 1.0 - w, 0.0) + jnp.where(slot_id == i1, w, 0.0)
        high = taps.astype(jnp.bfloat16)
        low = (taps - high.astype(jnp.float32)).astype(jnp.bfloat16)
        rows_o = lax.dot_general(
            jnp.concatenate([high, low], axis=0), received, (((0,), (0,)), ((), ())),
            preferred_element_type=jnp.float32)
        sr, si = rows_o[:, :128], rows_o[:, 128:]
        for p in range(PART_DEV):
            wr = weighted[half, p, :, :128].astype(jnp.float32)
            wi = weighted[half, p, :, 128:].astype(jnp.float32)
            product[buf, p * rows_u:(p + 1) * rows_u, :128] = (wr * sr + wi * si).astype(jnp.bfloat16)
            product[buf, p * rows_u:(p + 1) * rows_u, 128:] = (wr * si - wi * sr).astype(jnp.bfloat16)
        z = jnp.dot(product[buf], col_ph[half], preferred_element_type=jnp.float32)
        z = (z[:, :128] + z[:, 128:]).reshape(PART_DEV, rows_u, 128)
        return jnp.sum(z * row_ph[...][None], axis=1)

    partial = {}
    for turn, half in enumerate([1 - x, x]):
        for i in (0, 1) if turn == 0 else (2, 3):
            for ds in range(n_slab):
                if i < n_grp - 1 or ds > 0:
                    whose = (lax.rem(s + ds, n_slab), order[i])
                    row_copy(whose, whose).wait_recv()
        received = lists(half, turn)
        for i in range(n_grp):
            to_g = order[i]
            folded = []
            for e in range(2):
                o = to_g * 2 + e
                t = half_score(o, half, received, e)
                if turn == 0:
                    partial[i, e] = t
                else:
                    t = partial[i, e] + t
                    t = (t + pltpu.roll(t, 64, 1)) * (1.0 / NF)
                    folded.append(t)
            if turn == 1:
                part_send[to_g] = jnp.where(lane_p < 64, folded[0], folded[1])
                if i < n_grp - 1:
                    sum_copy(to_g, g).start()
    for dg, ds in peers:
        row_copy(peer(dg, ds), (s, g)).wait_send()
    total = part_send[g]
    for dg in range(1, n_grp):
        from_g = lax.rem(g + dg, n_grp)
        sum_copy(from_g, from_g).wait_recv()
        total += part_recv[from_g]
    out[...] = total
    listed_out[...] = jnp.where(g * (ORI_MAX // n_grp) + lane_p // TRANS < ori_count[...], 1, 0)
    for dg in range(1, n_grp):
        sum_copy(lax.rem(g + dg, n_grp), g).wait_send()


def maps_row(maps, s, g, n_slab):
    return jnp.concatenate([maps[g, a, pl.ds(s, 1), :] for a in range(n_slab)], axis=0)


def run_fused(n_slab, n_grp, cap, collective_id, args):
    pencils, send_map, index, frac, count, spectra, class_ids, ctf = args
    ky_loc, kx_loc = pencils.shape[:2]
    rows_u = spectra.shape[1]
    slots = n_slab * CAP
    chunks = ky_loc // 4
    vmem, smem = (pl.BlockSpec(memory_space=m) for m in (pltpu.VMEM, pltpu.SMEM))
    dma = pltpu.SemaphoreType.DMA
    return pl.pallas_call(
        lambda *refs: fused(n_slab, n_grp, cap, *refs),
        out_shape=[
            jax.ShapeDtypeStruct((PART_DEV, ORI_MAX * TRANS // n_grp), jnp.float32),
            jax.ShapeDtypeStruct((1,), jnp.int32),
            jax.ShapeDtypeStruct((PART_DEV, ORI_MAX * TRANS // n_grp), jnp.int32),
        ],
        in_specs=[pl.BlockSpec(memory_space=pltpu.HBM)] * 11,
        out_specs=[vmem, smem, vmem],
        scratch_shapes=[
            pltpu.VMEM((n_grp, n_slab, n_slab, slots), jnp.int32),
            pltpu.VMEM((chunks, 4, kx_loc, 2 * NF), jnp.float32),
            pltpu.VMEM((2 * NF, 2 * NF), jnp.bfloat16),
            pltpu.VMEM((ky_loc // 2, NF, 256), jnp.bfloat16),
            pltpu.VMEM(spectra.shape, jnp.bfloat16),
            pltpu.VMEM(ctf.shape, jnp.bfloat16),
            pltpu.VMEM((2, NF, 256), jnp.bfloat16),
            pltpu.VMEM((rows_u, 128), jnp.float32),
            pltpu.VMEM((n_grp, n_slab, slots), jnp.float32),
            pltpu.VMEM((n_grp, n_slab, slots), jnp.float32),
            pltpu.VMEM((2, 256, ky_loc // 2 * NF), jnp.bfloat16),
            pltpu.VMEM((n_grp, n_slab, cap, 128), jnp.bfloat16),
            pltpu.VMEM((n_grp, n_slab * cap, 128), jnp.bfloat16),
            pltpu.VMEM((2, PART_DEV, rows_u, NF), jnp.bfloat16),
            pltpu.VMEM((2, PART_DEV * rows_u, NF), jnp.bfloat16),
            pltpu.VMEM((n_grp, PART_DEV, 128), jnp.float32),
            pltpu.VMEM((n_grp, PART_DEV, 128), jnp.float32),
            pltpu.SMEM(class_ids.shape, jnp.int32),
            pltpu.VMEM((1, 1), jnp.int32),
            pltpu.VMEM(send_map.shape[2:], jnp.int32),
            pltpu.VMEM((2, ORI_MAX, rows_u), jnp.int32),
            pltpu.VMEM((ORI_MAX, rows_u), jnp.float32),
            dma((10,)),
            dma((chunks,)),
            dma((n_slab, n_grp)),
            dma((n_slab, n_grp)),
            dma((n_grp, n_slab)),
            dma((n_grp, n_slab)),
            dma((n_grp,)),
            dma((n_grp,)),
        ],
        compiler_params=pltpu.CompilerParams(
            collective_id=collective_id, has_side_effects=True, vmem_limit_bytes=60 * 2**20),
    )(
        class_ids, count.reshape(1, 1), send_map[0, 0], index[:, 0], frac[0], pencils, jnp.asarray(dft_table()),
        spectra, ctf, jnp.asarray(column_phases()), jnp.asarray(row_phases()),
    )


def listed(n_slab, n_grp, *args):
    scores, load, in_list = run_fused(n_slab, n_grp, CAP_FAST, 1, args)
    any_list = (*args[:4], jnp.zeros((1,), jnp.int32), *args[5:])
    chosen = lax.cond(
        load.reshape(()) > 0,
        lambda: run_fused(n_slab, n_grp, n_slab * CAP, 2, any_list)[0],
        lambda: scores,
    )
    return jnp.where(in_list > 0, chosen, 0.0)


def solution(mesh):
    n_slab, n_grp = mesh.shape["slab"], mesh.shape["grp"]

    def body(*args):
        if n_slab * CAP == 128 and n_grp == 4:
            return listed(n_slab, n_grp, *args)
        return shards(*args)

    return jax.shard_map(
        body,
        mesh=mesh,
        in_specs=(
            P("slab", "grp", None),
            P("slab", "grp", None, None),
            P(None, "slab", None, "grp"),
            P("slab", None, "grp"),
            P("slab"),
            P("slab", "grp", None),
            P("slab"),
            P(None, "grp", None),
        ),
        out_specs=P("slab", "grp"),
        check_vma=False,
    )
```
